256 devices in a mesh: wide: 64 (over y, z, x_lo), narrow: 4 (over x_hi, core).
Axes of the slice: x: 4 (x_hi: 2, x_lo: 2; x = x_hi * 2 + x_lo), y: 4, z: 8, core: 2. Of those that a mesh axis runs over, the one named last changes fastest.
Arguments:
- logits: bfloat16 [131072, 4096], P('wide', 'narrow'), may hold values from -9 to 280
- expression: bfloat16 [131072, 512], P('wide')
- measured: float32 [512, 4096], P('wide', 'narrow')
Outputs:
- grad_logits: bfloat16 [131072, 4096], P('wide', 'narrow')
- per_gene_similarity: float32 [512], P('wide')
The draws below stay inside these ranges and needn't reach their ends.
All inputs are finite; a program needn't handle non-finite values.
Results may differ from the reference program's by a relative error of at most 0.0054.
Values may be sent and summed in bfloat16 or wider, within the bound.
No kernel may reach another device: no remote copies, remote signals or barrier semaphores. Data moves between devices by JAX's collectives and lax.ppermute only.
A program may use at most 64 MiB of HBM per device.

```python
import math
import jax
import jax.numpy as jnp
from jax import lax

GENES = 512
CELL_DEV = 2048
CELLS = 131072
SPOTS = 4096


def cell_structure(key):
    key_list = jax.random.split(key, 3)
    cell_kind = jax.random.randint(key_list[0], (CELLS,), 0, 16)
    affinity = jnp.clip(0.9 * jax.random.normal(key_list[1], (16, SPOTS), jnp.float32), -2.7, 2.7)
    profile = jax.random.normal(key_list[2], (16, GENES), jnp.float32)
    return (cell_kind, affinity, profile)


def draw_logits(key, part):
    cell_kind, affinity, profile = cell_structure(key)
    key = jax.random.fold_in(key, 7)
    keys = jax.random.split(key, 1)
    values = jnp.clip(1.2 * jax.random.normal(keys[0], (CELLS, SPOTS), jnp.float32) + affinity[cell_kind], -9.0, 9.0)
    return values.astype(jnp.bfloat16)


def draw_expression(key, part):
    cell_kind, affinity, profile = cell_structure(key)
    key = jax.random.fold_in(key, 11)
    key_list = jax.random.split(key, 2)
    block_count = CELLS // CELL_DEV
    pairing = jax.random.permutation(key_list[0], block_count)
    cell_block = jnp.arange(CELLS, dtype=jnp.int32) // CELL_DEV
    gene_block = jnp.arange(GENES, dtype=jnp.int32) // (GENES // block_count)
    boosted = pairing[cell_block][:, None] == gene_block[None, :]
    jitter = jnp.clip(jax.random.normal(key_list[1], (CELLS, GENES), jnp.float32), -6.0, 6.0)
    strength = 8.2 / math.sqrt(CELLS)
    values = strength * profile[cell_kind] + jitter * jnp.where(boosted, 3.0, 1.0)
    return values.astype(jnp.bfloat16)


def draw_measured(key, part):
    cell_kind, affinity, profile = cell_structure(key)
    key = jax.random.fold_in(key, 13)
    weights = jnp.exp(affinity - 0.405)
    pattern = jnp.zeros((GENES, SPOTS), jnp.float32)
    for kind_index in range(16):
        pattern = pattern + profile[kind_index][:, None] * weights[kind_index][None, :]
    pattern = pattern / 6.0
    jitter = 0.5 * jnp.clip(jax.random.normal(key, (GENES, SPOTS), jnp.float32), -6.0, 6.0)
    return pattern + jitter


def setup_inputs(seed: int = 0) -> dict:
    splits = jax.random.split(jax.random.key(seed), 4)
    return {
        "logits": draw_logits(jax.random.fold_in(splits[3], 71), 0),
        "expression": draw_expression(jax.random.fold_in(splits[3], 71), 0),
        "measured": draw_measured(jax.random.fold_in(splits[3], 71), 0),
    }


def softmax_rows(block):
    values = block.astype(jnp.float32)
    top = lax.optimization_barrier(jnp.max(values, axis=1, keepdims=True))
    expo = jnp.exp(values - top)
    return expo / lax.optimization_barrier(jnp.sum(expo, axis=1, keepdims=True))

def reference(logits, expression, measured):
    count = CELLS // CELL_DEV
    logit_blocks = logits.reshape(count, CELL_DEV, SPOTS)
    expr_blocks = expression.reshape(count, CELL_DEV, GENES)

    def forward(total, pair):
        probs = softmax_rows(pair[0]).astype(jnp.bfloat16)
        return (total + jnp.dot(pair[1].T, probs, preferred_element_type=jnp.float32), None)
    predicted_expression, _ = lax.scan(forward, jnp.zeros((GENES, SPOTS), jnp.float32), (logit_blocks, expr_blocks))
    inner_product = lax.optimization_barrier(jnp.sum(predicted_expression * measured, axis=1))
    norm_p = jnp.sqrt(lax.optimization_barrier(jnp.sum(predicted_expression * predicted_expression, axis=1)) + 1e-06)
    measured_norm = jnp.sqrt(lax.optimization_barrier(jnp.sum(measured * measured, axis=1)) + 1e-06)
    per_gene_similarity = inner_product / (norm_p * measured_norm)
    d_pred = (-measured / (norm_p * measured_norm)[:, None] + (inner_product / (norm_p ** 3 * measured_norm))[:, None] * predicted_expression).astype(jnp.bfloat16)

    def backward(pair):
        probs = softmax_rows(pair[0])
        d_probs = jnp.dot(pair[1], d_pred, preferred_element_type=jnp.float32)
        row_dot = lax.optimization_barrier(jnp.sum(probs * d_probs, axis=1, keepdims=True))
        return (SPOTS * probs * (d_probs - row_dot)).astype(jnp.bfloat16)
    grads = lax.map(backward, (logit_blocks, expr_blocks))
    return (grads.reshape(CELLS, SPOTS), per_gene_similarity)
```

```python
import jax
import jax.numpy as jnp
from jax import lax
from jax.sharding import PartitionSpec as P

Y, Z, X, R = 4, 8, 2, 8


def wide_index(y, z, x):
    return (y * Z + z) * X + x


YX_GROUPS = [[wide_index(y, z, x) for y in range(Y) for x in range(X)] for z in range(Z)]
Z_GROUPS = [[wide_index(y, z, x) for z in range(Z)] for y in range(Y) for x in range(X)]


def swap(v, groups):
    return lax.all_to_all(v, "wide", 0, 0, axis_index_groups=groups)


def narrow_peers(v):
    return [lax.ppermute(v, "narrow", [(i, i ^ d) for i in range(4)]) for d in (3, 2, 1)]


def body(logits, expression, measured):
    spots = logits.shape[1]
    values = logits.astype(jnp.float32)
    local_top = jnp.max(values, axis=1)
    local_log = local_top + jnp.log(jnp.sum(jnp.exp(values - local_top[:, None]), axis=1))
    logs = [local_log] + narrow_peers(local_log)
    top = jnp.maximum(jnp.maximum(logs[0], logs[1]), jnp.maximum(logs[2], logs[3]))
    log_total = top + jnp.log(sum(jnp.exp(v - top) for v in logs))
    probs = jnp.exp(values - log_total[:, None])
    probs_low = probs.astype(jnp.bfloat16)
    part = lax.dot_general(
        expression, probs_low, (((0,), (0,)), ((), ())), preferred_element_type=jnp.float32
    ).astype(jnp.bfloat16)
    part = part.reshape(Y, Z, X, R, spots).transpose(0, 2, 1, 3, 4).reshape(Y * X, Z * R, spots)
    part = swap(part, YX_GROUPS).astype(jnp.float32).sum(0).astype(jnp.bfloat16)
    part = swap(part.reshape(Z, R, spots), Z_GROUPS)
    predicted = part.astype(jnp.float32).sum(0)
    sums = jnp.stack(
        [
            jnp.sum(predicted * measured, axis=1),
            jnp.sum(predicted * predicted, axis=1),
            jnp.sum(measured * measured, axis=1),
        ]
    )
    sums = sums + sum(narrow_peers(sums))
    inner, pred_sq, meas_sq = sums[0], sums[1], sums[2]
    norm_p = jnp.sqrt(pred_sq + 1e-06)
    norm_m = jnp.sqrt(meas_sq + 1e-06)
    similarity = inner / (norm_p * norm_m)
    share = (
        -measured / (norm_p * norm_m)[:, None]
        + (inner / (norm_p**3 * norm_m))[:, None] * predicted
    ).astype(jnp.bfloat16)
    share = swap(jnp.broadcast_to(share[None], (Z, R, spots)), Z_GROUPS).reshape(Z * R, spots)
    share = swap(jnp.broadcast_to(share[None], (Y * X, Z * R, spots)), YX_GROUPS)
    d_pred = share.reshape(Y, X, Z, R, spots).transpose(0, 2, 1, 3, 4).reshape(Y * X * Z * R, spots)
    d_probs = jnp.dot(expression, d_pred, preferred_element_type=jnp.float32)
    row_dot = jnp.sum(probs * d_probs, axis=1)
    row_dot = row_dot + sum(narrow_peers(row_dot))
    total_spots = spots * lax.axis_size("narrow")
    grad = (total_spots * probs * (d_probs - row_dot[:, None])).astype(jnp.bfloat16)
    return (grad, similarity)


def solution(mesh):
    placed = (P("wide", "narrow"), P("wide", None), P("wide", "narrow"))
    return jax.shard_map(
        body,
        mesh=mesh,
        in_specs=placed,
        out_specs=(P("wide", "narrow"), P("wide")),
        check_vma=False,
    )
```

```python
import functools

import jax
import jax.numpy as jnp
from jax import lax
from jax.experimental import pallas as pl
from jax.experimental.pallas import tpu as pltpu
from jax.sharding import PartitionSpec as P

Y, Z, X, R = 4, 8, 2, 8
LANES = 128
ROWS = 256
MIB = 1 << 20


def wide_index(y, z, x):
    return (y * Z + z) * X + x


YX_GROUPS = [[wide_index(y, z, x) for y in range(Y) for x in range(X)] for z in range(Z)]
Z_GROUPS = [[wide_index(y, z, x) for z in range(Z)] for y in range(Y) for x in range(X)]


def swap(v, groups):
    return lax.all_to_all(v, "wide", 0, 0, axis_index_groups=groups)


def narrow_peers(v):
    return [lax.ppermute(v, "narrow", [(i, i ^ d) for i in range(4)]) for d in (3, 2, 1)]


def fold(parts, op):
    parts = list(parts)
    while len(parts) > 1:
        parts = [op(a, b) for a, b in zip(parts[::2], parts[1::2])]
    return parts[0]


def lane_groups(width):
    return [slice(k, k + LANES) for k in range(0, width, LANES)]


def as_row(column_sums):
    return jnp.sum(column_sums.T, axis=0, keepdims=True)


def as_column(row):
    return jnp.broadcast_to(row, (LANES, row.shape[1])).T


def stats_kernel(x_ref, out_ref):
    step = pl.program_id(0)
    groups = lane_groups(x_ref.shape[1])
    top = fold([x_ref[:, g] for g in groups], jnp.maximum).astype(jnp.float32)
    top = jnp.broadcast_to(jnp.max(top, axis=1, keepdims=True), top.shape)
    total = fold([jnp.exp(x_ref[:, g].astype(jnp.float32) - top) for g in groups], jnp.add)
    out_ref[pl.ds(step, 1), :] = top.T[:1] + jnp.log(as_row(total))


def forward_kernel(x_ref, e_ref, log_ref, out_ref, low, acc):
    step = pl.program_id(0)
    log_total = as_column(log_ref[pl.ds(step, 1), :])
    for g in lane_groups(x_ref.shape[1]):
        low[:, g] = jnp.exp(x_ref[:, g].astype(jnp.float32) - log_total).astype(jnp.bfloat16)
    part = lax.dot_general(
        e_ref[...], low[...], (((0,), (0,)), ((), ())), preferred_element_type=jnp.float32
    )

    @pl.when(step == 0)
    def _():
        acc[...] = part

    @pl.when(step > 0)
    def _():
        acc[...] += part

    @pl.when(step == pl.num_programs(0) - 1)
    def _():
        out_ref[...] = acc[...].astype(jnp.bfloat16)


def backward_kernel(x_ref, e_ref, d_ref, log_ref, probs_ref, dprobs_ref, dot_ref):
    step = pl.program_id(0)
    log_total = as_column(log_ref[pl.ds(step, 1), :])
    dprobs_ref[...] = jnp.dot(e_ref[...], d_ref[...], preferred_element_type=jnp.float32)
    parts = []
    for g in lane_groups(x_ref.shape[1]):
        probs = jnp.exp(x_ref[:, g].astype(jnp.float32) - log_total)
        probs_ref[:, g] = probs
        parts.append(probs * dprobs_ref[:, g])
    dot_ref[pl.ds(step, 1), :] = as_row(fold(parts, jnp.add))


def gradient_kernel(scale, probs_ref, dprobs_ref, dot_ref, out_ref):
    step = pl.program_id(0)
    row_dot = as_column(dot_ref[pl.ds(step, 1), :])
    for g in lane_groups(probs_ref.shape[1]):
        out_ref[:, g] = (scale * probs_ref[:, g] * (dprobs_ref[:, g] - row_dot)).astype(jnp.bfloat16)


def row_block(width):
    return pl.BlockSpec((ROWS, width), lambda i: (i, 0))


def whole(*shape):
    return pl.BlockSpec(shape, lambda i: (0,) * len(shape))


def params(mib):
    return pltpu.CompilerParams(dimension_semantics=("arbitrary",), vmem_limit_bytes=mib * MIB)


def local_log_sum(logits):
    cells, spots = logits.shape
    steps = cells // ROWS
    return pl.pallas_call(
        stats_kernel,
        grid=(steps,),
        in_specs=[row_block(spots)],
        out_specs=whole(steps, ROWS),
        out_shape=jax.ShapeDtypeStruct((steps, ROWS), jnp.float32),
        compiler_params=params(8),
        name="stats",
    )(logits)


def partial_predicted(logits, expression, log_total):
    cells, spots = logits.shape
    genes = expression.shape[1]
    steps = cells // ROWS
    return pl.pallas_call(
        forward_kernel,
        grid=(steps,),
        in_specs=[row_block(spots), row_block(genes), whole(steps, ROWS)],
        out_specs=whole(genes, spots),
        out_shape=jax.ShapeDtypeStruct((genes, spots), jnp.bfloat16),
        scratch_shapes=[
            pltpu.VMEM((ROWS, spots), jnp.bfloat16),
            pltpu.VMEM((genes, spots), jnp.float32),
        ],
        compiler_params=params(16),
        name="forward",
    )(logits, expression, log_total)


def backward(logits, expression, d_pred, log_total):
    cells, spots = logits.shape
    genes = expression.shape[1]
    steps = cells // ROWS
    return pl.pallas_call(
        backward_kernel,
        grid=(steps,),
        in_specs=[row_block(spots), row_block(genes), whole(genes, spots), whole(steps, ROWS)],
        out_specs=[row_block(spots), row_block(spots), whole(steps, ROWS)],
        out_shape=[
            jax.ShapeDtypeStruct((cells, spots), jnp.float32),
            jax.ShapeDtypeStruct((cells, spots), jnp.float32),
            jax.ShapeDtypeStruct((steps, ROWS), jnp.float32),
        ],
        compiler_params=params(16),
        name="backward",
    )(logits, expression, d_pred, log_total)


def gradient(probs, d_probs, row_dot, scale):
    cells, spots = probs.shape
    steps = cells // ROWS
    return pl.pallas_call(
        functools.partial(gradient_kernel, scale),
        grid=(steps,),
        in_specs=[row_block(spots), row_block(spots), whole(steps, ROWS)],
        out_specs=row_block(spots),
        out_shape=jax.ShapeDtypeStruct((cells, spots), jnp.bfloat16),
        compiler_params=params(16),
        name="gradient",
    )(probs, d_probs, row_dot)


def body(logits, expression, measured):
    spots = logits.shape[1]
    local_log = local_log_sum(logits)
    logs = [local_log] + narrow_peers(local_log)
    top = fold(logs, jnp.maximum)
    log_total = top + jnp.log(fold([jnp.exp(v - top) for v in logs], jnp.add))
    part = partial_predicted(logits, expression, log_total)
    part = part.reshape(Y, Z, X, R, spots).transpose(0, 2, 1, 3, 4).reshape(Y * X, Z * R, spots)
    part = swap(part, YX_GROUPS).astype(jnp.float32).sum(0).astype(jnp.bfloat16)
    part = swap(part.reshape(Z, R, spots), Z_GROUPS)
    predicted = part.astype(jnp.float32).sum(0)
    sums = jnp.stack(
        [
            jnp.sum(predicted * measured, axis=1),
            jnp.sum(predicted * predicted, axis=1),
            jnp.sum(measured * measured, axis=1),
        ]
    )
    sums = sums + fold([jnp.zeros_like(sums)] + narrow_peers(sums), jnp.add)
    inner, pred_sq, meas_sq = sums[0], sums[1], sums[2]
    norm_p = jnp.sqrt(pred_sq + 1e-06)
    norm_m = jnp.sqrt(meas_sq + 1e-06)
    similarity = inner / (norm_p * norm_m)
    share = (
        -measured / (norm_p * norm_m)[:, None]
        + (inner / (norm_p**3 * norm_m))[:, None] * predicted
    ).astype(jnp.bfloat16)
    share = swap(jnp.broadcast_to(share[None], (Z, R, spots)), Z_GROUPS).reshape(Z * R, spots)
    share = swap(jnp.broadcast_to(share[None], (Y * X, Z * R, spots)), YX_GROUPS)
    d_pred = share.reshape(Y, X, Z, R, spots).transpose(0, 2, 1, 3, 4).reshape(Y * X * Z * R, spots)
    probs, d_probs, row_dot = backward(logits, expression, d_pred, log_total)
    row_dot = fold([row_dot] + narrow_peers(row_dot), jnp.add)
    grad = gradient(probs, d_probs, row_dot, float(spots * lax.axis_size("narrow")))
    return (grad, similarity)


def solution(mesh):
    placed = (P("wide", "narrow"), P("wide", None), P("wide", "narrow"))
    return jax.shard_map(
        body,
        mesh=mesh,
        in_specs=placed,
        out_specs=(P("wide", "narrow"), P("wide")),
        check_vma=False,
    )
```

```python
import functools

import jax
import jax.numpy as jnp
from jax import lax
from jax.experimental import pallas as pl
from jax.experimental.pallas import tpu as pltpu
from jax.sharding import PartitionSpec as P

Y, Z, X, R = 4, 8, 2, 8
LANES = 128
ROWS = 256
STATS_MIB = 58
MIB = 1 << 20


def wide_index(y, z, x):
    return (y * Z + z) * X + x


YX_GROUPS = [[wide_index(y, z, x) for y in range(Y) for x in range(X)] for z in range(Z)]
Z_GROUPS = [[wide_index(y, z, x) for z in range(Z)] for y in range(Y) for x in range(X)]


def swap(v, groups):
    return lax.all_to_all(v, "wide", 0, 0, axis_index_groups=groups)


def narrow_peers(v):
    return [lax.ppermute(v, "narrow", [(i, i ^ d) for i in range(4)]) for d in (3, 2, 1)]


def fold(parts, op):
    parts = list(parts)
    while len(parts) > 1:
        parts = [op(a, b) for a, b in zip(parts[::2], parts[1::2])]
    return parts[0]


def lane_groups(width):
    return [slice(k, k + LANES) for k in range(0, width, LANES)]


def as_row(column_sums):
    return jnp.sum(column_sums.T, axis=0, keepdims=True)


def as_column(row):
    return jnp.broadcast_to(row, (LANES, row.shape[1])).T


def block(i):
    return pl.ds(pl.multiple_of(i * ROWS, ROWS), ROWS)


def stats_kernel(x_hbm, out_ref, x_ref, sems):
    cells, spots = x_ref.shape
    steps = cells // ROWS
    groups = lane_groups(spots)

    def copy(i):
        return pltpu.make_async_copy(x_hbm.at[block(i), :], x_ref.at[block(i), :], sems.at[i])

    for i in range(steps):
        copy(i).start()

    @pl.loop(0, steps)
    def _(i):
        copy(i).wait()
        rows = block(i)
        top = fold([x_ref[rows, g] for g in groups], jnp.maximum).astype(jnp.float32)
        total = fold([jnp.exp(x_ref[rows, g].astype(jnp.float32) - top) for g in groups], jnp.add)
        top, total = top.T, total.T
        row_top = jnp.max(top, axis=0, keepdims=True)
        row_total = jnp.sum(total * jnp.exp(top - row_top), axis=0, keepdims=True)
        out_ref[pl.ds(i, 1), :] = row_top + jnp.log(row_total)


def transpose_kernel(e_ref, out_ref):
    @pl.loop(0, e_ref.shape[0] // ROWS)
    def _(i):
        out_ref[:, block(i)] = e_ref[block(i), :].T


def forward_kernel(tile, x_ref, et_ref, log_ref, part_ref, probs_ref, low, column):
    cells, spots = x_ref.shape

    @pl.loop(0, cells // ROWS)
    def _(i):
        column[block(i), :] = as_column(log_ref[pl.ds(i, 1), :])

    tiles = [slice(k, k + tile) for k in range(0, spots, tile)]

    def fill(cols):
        for k in range(cols.start, cols.stop, LANES):
            g = slice(k, k + LANES)
            probs = jnp.exp(x_ref[:, g].astype(jnp.float32) - column[...])
            probs_ref[:, g] = probs
            low[:, g] = probs.astype(jnp.bfloat16)

    fill(tiles[0])
    for cols, later in zip(tiles, tiles[1:] + [None]):
        part = jnp.dot(et_ref[...], low[:, cols], preferred_element_type=jnp.float32)
        part_ref[:, cols] = part.astype(jnp.bfloat16)
        if later is not None:
            fill(later)


def backward_kernel(size, probs_ref, e_ref, d_ref, dprobs_ref, dot_ref):
    cells, spots = probs_ref.shape

    def row_dots(first):
        for k in range(first, first + size, ROWS):
            rows = slice(k, k + ROWS)
            parts = [probs_ref[rows, g] * dprobs_ref[rows, g] for g in lane_groups(spots)]
            dot_ref[k // ROWS : k // ROWS + 1, :] = as_row(fold(parts, jnp.add))

    for first in range(0, cells, size):
        rows = slice(first, first + size)
        dprobs_ref[rows, :] = jnp.dot(e_ref[rows, :], d_ref[...], preferred_element_type=jnp.float32)
        if first:
            row_dots(first - size)
    row_dots(cells - size)


def gradient_kernel(scale, size, probs_ref, dprobs_ref, dot_ref, out_hbm, buf, sems):
    cells, spots = probs_ref.shape
    steps = cells // size
    inner = size // ROWS

    def copy(i):
        rows = pl.ds(pl.multiple_of(i * size, size), size)
        return pltpu.make_async_copy(buf.at[rows, :], out_hbm.at[rows, :], sems.at[i])

    @pl.loop(0, steps)
    def _(i):
        for h in range(inner):
            rows = block(i * inner + h)
            row_dot = as_column(dot_ref[pl.ds(i * inner + h, 1), :])
            for g in lane_groups(spots):
                grad = scale * probs_ref[rows, g] * (dprobs_ref[rows, g] - row_dot)
                buf[rows, g] = grad.astype(jnp.bfloat16)
        copy(i).start()

    for i in range(steps):
        copy(i).wait()


VMEM = pl.BlockSpec(memory_space=pltpu.VMEM)
HBM = pl.BlockSpec(memory_space=pltpu.HBM)


def params(mib):
    return pltpu.CompilerParams(vmem_limit_bytes=mib * MIB)


def cost(flops, moved, transcendentals=0):
    return pl.CostEstimate(flops=flops, bytes_accessed=moved, transcendentals=transcendentals)


def local_log_sum(logits):
    cells, spots = logits.shape
    steps = cells // ROWS
    return pl.pallas_call(
        stats_kernel,
        in_specs=[HBM],
        out_specs=VMEM,
        out_shape=jax.ShapeDtypeStruct((steps, ROWS), jnp.float32),
        scratch_shapes=[
            pltpu.VMEM((cells, spots), logits.dtype),
            pltpu.SemaphoreType.DMA((steps,)),
        ],
        compiler_params=params(STATS_MIB),
        cost_estimate=cost(cells * spots * 6, cells * spots * 2, cells * spots),
        name="stats",
    )(logits)


def transposed(expression):
    cells, genes = expression.shape
    return pl.pallas_call(
        transpose_kernel,
        in_specs=[VMEM],
        out_specs=VMEM,
        out_shape=jax.ShapeDtypeStruct((genes, cells), expression.dtype),
        compiler_params=params(8),
        cost_estimate=cost(0, cells * genes * 4),
        name="transpose",
    )(expression)


def partial_predicted(logits, expression_t, log_total):
    cells, spots = logits.shape
    genes = expression_t.shape[0]
    return pl.pallas_call(
        functools.partial(forward_kernel, 256),
        in_specs=[VMEM] * 3,
        out_specs=[VMEM] * 2,
        out_shape=[
            jax.ShapeDtypeStruct((genes, spots), jnp.bfloat16),
            jax.ShapeDtypeStruct((cells, spots), jnp.float32),
        ],
        scratch_shapes=[
            pltpu.VMEM((cells, spots), jnp.bfloat16),
            pltpu.VMEM((cells, LANES), jnp.float32),
        ],
        compiler_params=params(24),
        cost_estimate=cost(2 * cells * spots * genes, cells * spots * 4, cells * spots),
        name="forward",
    )(logits, expression_t, log_total)


def backward(probs, expression, d_pred):
    cells, spots = probs.shape
    genes = expression.shape[1]
    return pl.pallas_call(
        functools.partial(backward_kernel, 512),
        in_specs=[VMEM] * 3,
        out_specs=[VMEM] * 2,
        out_shape=[
            jax.ShapeDtypeStruct((cells, spots), jnp.float32),
            jax.ShapeDtypeStruct((cells // ROWS, ROWS), jnp.float32),
        ],
        compiler_params=params(12),
        cost_estimate=cost(2 * cells * spots * genes, cells * spots * 4),
        name="backward",
    )(probs, expression, d_pred)


def gradient(probs, d_probs, row_dot, scale):
    cells, spots = probs.shape
    size = 512
    return pl.pallas_call(
        functools.partial(gradient_kernel, scale, size),
        in_specs=[VMEM] * 3,
        out_specs=HBM,
        out_shape=jax.ShapeDtypeStruct((cells, spots), jnp.bfloat16),
        scratch_shapes=[
            pltpu.VMEM((cells, spots), jnp.bfloat16),
            pltpu.SemaphoreType.DMA((cells // size,)),
        ],
        compiler_params=params(12),
        cost_estimate=cost(cells * spots * 3, cells * spots * 4),
        name="gradient",
    )(probs, d_probs, row_dot)


def body(logits, expression, measured):
    spots = logits.shape[1]
    local_log = local_log_sum(logits)
    expression_t = transposed(expression)
    logs = [local_log] + narrow_peers(local_log)
    top = fold(logs, jnp.maximum)
    log_total = top + jnp.log(fold([jnp.exp(v - top) for v in logs], jnp.add))
    part, probs = partial_predicted(logits, expression_t, log_total)
    part = part.reshape(Y, Z, X, R, spots).transpose(0, 2, 1, 3, 4).reshape(Y * X, Z * R, spots)
    part = swap(part, YX_GROUPS).astype(jnp.float32).sum(0).astype(jnp.bfloat16)
    part = swap(part.reshape(Z, R, spots), Z_GROUPS)
    predicted = part.astype(jnp.float32).sum(0)
    sums = jnp.stack(
        [
            jnp.sum(predicted * measured, axis=1),
            jnp.sum(predicted * predicted, axis=1),
            jnp.sum(measured * measured, axis=1),
        ]
    )
    sums = sums + fold([jnp.zeros_like(sums)] + narrow_peers(sums), jnp.add)
    inner, pred_sq, meas_sq = sums[0], sums[1], sums[2]
    norm_p = jnp.sqrt(pred_sq + 1e-06)
    norm_m = jnp.sqrt(meas_sq + 1e-06)
    similarity = inner / (norm_p * norm_m)
    share = (
        -measured / (norm_p * norm_m)[:, None]
        + (inner / (norm_p**3 * norm_m))[:, None] * predicted
    ).astype(jnp.bfloat16)
    share = swap(jnp.broadcast_to(share[None], (Z, R, spots)), Z_GROUPS).reshape(Z * R, spots)
    share = swap(jnp.broadcast_to(share[None], (Y * X, Z * R, spots)), YX_GROUPS)
    d_pred = share.reshape(Y, X, Z, R, spots).transpose(0, 2, 1, 3, 4).reshape(Y * X * Z * R, spots)
    d_probs, row_dot = backward(probs, expression, d_pred)
    row_dot = fold([row_dot] + narrow_peers(row_dot), jnp.add)
    grad = gradient(probs, d_probs, row_dot, float(spots * lax.axis_size("narrow")))
    return (grad, similarity)


def solution(mesh):
    placed = (P("wide", "narrow"), P("wide", None), P("wide", "narrow"))
    return jax.shard_map(
        body,
        mesh=mesh,
        in_specs=placed,
        out_specs=(P("wide", "narrow"), P("wide")),
        check_vma=False,
    )
```

```python
import functools

import jax
import jax.numpy as jnp
from jax import lax
from jax.experimental import pallas as pl
from jax.experimental.pallas import tpu as pltpu
from jax.sharding import PartitionSpec as P

Y, Z, X, R = 4, 8, 2, 8
LANES = 128
ROWS = 256
STATS_MIB = 60
MIB = 1 << 20


def wide_index(y, z, x):
    return (y * Z + z) * X + x


YX_GROUPS = [[wide_index(y, z, x) for y in range(Y) for x in range(X)] for z in range(Z)]
Z_GROUPS = [[wide_index(y, z, x) for z in range(Z)] for y in range(Y) for x in range(X)]


def swap(v, groups):
    return lax.all_to_all(v, "wide", 0, 0, axis_index_groups=groups)


def narrow_combine(v, op):
    for d in (1, 2):
        v = op(v, lax.ppermute(v, "narrow", [(i, i ^ d) for i in range(4)]))
    return v


def log_add(a, b):
    top = jnp.maximum(a, b)
    return top + jnp.log(jnp.exp(a - top) + jnp.exp(b - top))


def fold(parts, op):
    parts = list(parts)
    while len(parts) > 1:
        parts = [op(a, b) for a, b in zip(parts[::2], parts[1::2])]
    return parts[0]


def lane_groups(width):
    return [slice(k, k + LANES) for k in range(0, width, LANES)]


def as_row(column_sums):
    return jnp.sum(column_sums.T, axis=0, keepdims=True)


def as_column(row):
    return jnp.broadcast_to(row, (LANES, row.shape[1])).T


def block(i):
    return pl.ds(pl.multiple_of(i * ROWS, ROWS), ROWS)


def stats_kernel(x_hbm, out_ref, x_ref, sems):
    cells, spots = x_ref.shape
    steps = cells // ROWS
    groups = lane_groups(spots)

    def copy(i):
        return pltpu.make_async_copy(x_hbm.at[block(i), :], x_ref.at[block(i), :], sems.at[i])

    for i in range(steps):
        copy(i).start()

    @pl.loop(0, steps)
    def _(i):
        copy(i).wait()
        rows = block(i)
        top = fold([x_ref[rows, g] for g in groups], jnp.maximum).astype(jnp.float32)
        total = fold([jnp.exp(x_ref[rows, g].astype(jnp.float32) - top) for g in groups], jnp.add)
        top, total = top.T, total.T
        row_top = jnp.max(top, axis=0, keepdims=True)
        row_total = jnp.sum(total * jnp.exp(top - row_top), axis=0, keepdims=True)
        out_ref[pl.ds(i, 1), :] = row_top + jnp.log(row_total)


def transpose_kernel(e_ref, out_ref):
    @pl.loop(0, e_ref.shape[0] // ROWS)
    def _(i):
        out_ref[:, block(i)] = e_ref[block(i), :].T


def forward_kernel(tile, x_ref, et_ref, log_ref, part_ref, low, column):
    cells, spots = x_ref.shape

    @pl.loop(0, cells // ROWS)
    def _(i):
        column[block(i), :] = as_column(log_ref[pl.ds(i, 1), :])

    tiles = [slice(k, k + tile) for k in range(0, spots, tile)]

    def fill(cols):
        for k in range(cols.start, cols.stop, LANES):
            g = slice(k, k + LANES)
            probs = jnp.exp(x_ref[:, g].astype(jnp.float32) - column[...])
            low[:, g] = probs.astype(jnp.bfloat16)

    fill(tiles[0])
    for cols, later in zip(tiles, tiles[1:] + [None]):
        part = jnp.dot(et_ref[...], low[:, cols], preferred_element_type=jnp.float32)
        part_ref[:, cols] = part.astype(jnp.bfloat16)
        if later is not None:
            fill(later)


def backward_kernel(size, x_ref, e_ref, d_ref, log_ref, probs_ref, dprobs_ref, dot_ref):
    cells, spots = probs_ref.shape

    def fill(first):
        for k in range(first, first + size, ROWS):
            rows = slice(k, k + ROWS)
            log_total = as_column(log_ref[k // ROWS : k // ROWS + 1, :])
            for g in lane_groups(spots):
                probs_ref[rows, g] = jnp.exp(x_ref[rows, g].astype(jnp.float32) - log_total)

    def row_dots(first):
        for k in range(first, first + size, ROWS):
            rows = slice(k, k + ROWS)
            parts = [probs_ref[rows, g] * dprobs_ref[rows, g] for g in lane_groups(spots)]
            dot_ref[k // ROWS : k // ROWS + 1, :] = as_row(fold(parts, jnp.add))

    for first in range(0, cells, size):
        rows = slice(first, first + size)
        dprobs_ref[rows, :] = jnp.dot(e_ref[rows, :], d_ref[...], preferred_element_type=jnp.float32)
        fill(first)
        if first:
            row_dots(first - size)
    row_dots(cells - size)


def gradient_kernel(scale, size, probs_ref, dprobs_ref, dot_ref, out_hbm, buf, sems):
    cells, spots = probs_ref.shape
    steps = cells // size
    inner = size // ROWS

    def copy(i):
        rows = pl.ds(pl.multiple_of(i * size, size), size)
        return pltpu.make_async_copy(buf.at[rows, :], out_hbm.at[rows, :], sems.at[i])

    @pl.loop(0, steps)
    def _(i):
        for h in range(inner):
            rows = block(i * inner + h)
            row_dot = as_column(dot_ref[pl.ds(i * inner + h, 1), :])
            for g in lane_groups(spots):
                grad = scale * probs_ref[rows, g] * (dprobs_ref[rows, g] - row_dot)
                buf[rows, g] = grad.astype(jnp.bfloat16)
        copy(i).start()

    for i in range(steps):
        copy(i).wait()


VMEM = pl.BlockSpec(memory_space=pltpu.VMEM)
HBM = pl.BlockSpec(memory_space=pltpu.HBM)


def params(mib):
    return pltpu.CompilerParams(vmem_limit_bytes=mib * MIB)


def cost(flops, moved, transcendentals=0):
    return pl.CostEstimate(flops=flops, bytes_accessed=moved, transcendentals=transcendentals)


def local_log_sum(logits):
    cells, spots = logits.shape
    steps = cells // ROWS
    return pl.pallas_call(
        stats_kernel,
        in_specs=[HBM],
        out_specs=VMEM,
        out_shape=jax.ShapeDtypeStruct((steps, ROWS), jnp.float32),
        scratch_shapes=[
            pltpu.VMEM((cells, spots), logits.dtype),
            pltpu.SemaphoreType.DMA((steps,)),
        ],
        compiler_params=params(STATS_MIB),
        cost_estimate=cost(cells * spots * 6, cells * spots * 2, cells * spots),
        name="stats",
    )(logits)


def transposed(expression):
    cells, genes = expression.shape
    return pl.pallas_call(
        transpose_kernel,
        in_specs=[VMEM],
        out_specs=VMEM,
        out_shape=jax.ShapeDtypeStruct((genes, cells), expression.dtype),
        compiler_params=params(8),
        cost_estimate=cost(0, cells * genes * 4),
        name="transpose",
    )(expression)


def partial_predicted(logits, expression_t, log_total):
    cells, spots = logits.shape
    genes = expression_t.shape[0]
    return pl.pallas_call(
        functools.partial(forward_kernel, 256),
        in_specs=[VMEM] * 3,
        out_specs=VMEM,
        out_shape=jax.ShapeDtypeStruct((genes, spots), jnp.bfloat16),
        scratch_shapes=[
            pltpu.VMEM((cells, spots), jnp.bfloat16),
            pltpu.VMEM((cells, LANES), jnp.float32),
        ],
        compiler_params=params(16),
        cost_estimate=cost(2 * cells * spots * genes, cells * spots * 4, cells * spots),
        name="forward",
    )(logits, expression_t, log_total)


def backward(logits, expression, d_pred, log_total):
    cells, spots = logits.shape
    genes = expression.shape[1]
    return pl.pallas_call(
        functools.partial(backward_kernel, 512),
        in_specs=[VMEM] * 4,
        out_specs=[VMEM] * 3,
        out_shape=[
            jax.ShapeDtypeStruct((cells, spots), jnp.float32),
            jax.ShapeDtypeStruct((cells, spots), jnp.float32),
            jax.ShapeDtypeStruct((cells // ROWS, ROWS), jnp.float32),
        ],
        compiler_params=params(12),
        cost_estimate=cost(2 * cells * spots * genes, cells * spots * 4, cells * spots),
        name="backward",
    )(logits, expression, d_pred, log_total)


def gradient(probs, d_probs, row_dot, scale):
    cells, spots = probs.shape
    size = 512
    return pl.pallas_call(
        functools.partial(gradient_kernel, scale, size),
        in_specs=[VMEM] * 3,
        out_specs=HBM,
        out_shape=jax.ShapeDtypeStruct((cells, spots), jnp.bfloat16),
        scratch_shapes=[
            pltpu.VMEM((cells, spots), jnp.bfloat16),
            pltpu.SemaphoreType.DMA((cells // size,)),
        ],
        compiler_params=params(12),
        cost_estimate=cost(cells * spots * 3, cells * spots * 4),
        name="gradient",
    )(probs, d_probs, row_dot)


def body(logits, expression, measured):
    spots = logits.shape[1]
    local_log = local_log_sum(logits)
    expression_t = transposed(expression)
    log_total = narrow_combine(local_log, log_add)
    part = partial_predicted(logits, expression_t, log_total)
    part = part.reshape(Y, Z, X, R, spots).transpose(0, 2, 1, 3, 4).reshape(Y * X, Z * R, spots)
    part = swap(part, YX_GROUPS).astype(jnp.float32).sum(0).astype(jnp.bfloat16)
    part = swap(part.reshape(Z, R, spots), Z_GROUPS)
    predicted = part.astype(jnp.float32).sum(0)
    sums = jnp.stack(
        [
            jnp.sum(predicted * measured, axis=1),
            jnp.sum(predicted * predicted, axis=1),
            jnp.sum(measured * measured, axis=1),
        ]
    )
    sums = narrow_combine(sums, jnp.add)
    inner, pred_sq, meas_sq = sums[0], sums[1], sums[2]
    norm_p = jnp.sqrt(pred_sq + 1e-06)
    norm_m = jnp.sqrt(meas_sq + 1e-06)
    similarity = inner / (norm_p * norm_m)
    share = (
        -measured / (norm_p * norm_m)[:, None]
        + (inner / (norm_p**3 * norm_m))[:, None] * predicted
    ).astype(jnp.bfloat16)
    share = swap(jnp.broadcast_to(share[None], (Z, R, spots)), Z_GROUPS).reshape(Z * R, spots)
    share = swap(jnp.broadcast_to(share[None], (Y * X, Z * R, spots)), YX_GROUPS)
    d_pred = share.reshape(Y, X, Z, R, spots).transpose(0, 2, 1, 3, 4).reshape(Y * X * Z * R, spots)
    probs, d_probs, row_dot = backward(logits, expression, d_pred, log_total)
    row_dot = narrow_combine(row_dot, jnp.add)
    grad = gradient(probs, d_probs, row_dot, float(spots * lax.axis_size("narrow")))
    return (grad, similarity)


def solution(mesh):
    placed = (P("wide", "narrow"), P("wide", None), P("wide", "narrow"))
    return jax.shard_map(
        body,
        mesh=mesh,
        in_specs=placed,
        out_specs=(P("wide", "narrow"), P("wide")),
        check_vma=False,
    )
```

```python
import functools

import jax
import jax.numpy as jnp
from jax import lax
from jax.experimental import pallas as pl
from jax.experimental.pallas import tpu as pltpu
from jax.sharding import PartitionSpec as P

Y, Z, X, R, N = 4, 8, 2, 8, 4
LANES = 128
ROWS = 256
MIB = 1 << 20


def wide_index(y, z, x):
    return (y * Z + z) * X + x


def device_index(y, z, x, n):
    return wide_index(y, z, x) * N + n


def yx_groups(n):
    return [[device_index(y, z, x, n) for y in range(Y) for x in range(X)] for z in range(Z)]


def z_groups(n):
    return [[device_index(y, z, x, n) for z in range(Z)] for y in range(Y) for x in range(X)]


WIDE_STAGE = [g for n in range(N) for g in (z_groups(n) if n % 2 else yx_groups(n))]
SHORT_STAGE = [g for n in range(N) for g in (yx_groups(n) if n % 2 else z_groups(n))]


def swap(v, groups):
    return lax.all_to_all(v, ("wide", "narrow"), 0, 0, axis_index_groups=groups)


def by_core(even, odd):
    return jnp.where(lax.axis_index("narrow") % 2 == 0, even, odd)


def narrow_combine(v, op):
    for d in (1, 2):
        v = op(v, lax.ppermute(v, "narrow", [(i, i ^ d) for i in range(4)]))
    return v


def log_add(a, b):
    top = jnp.maximum(a, b)
    return top + jnp.log(jnp.exp(a - top) + jnp.exp(b - top))


def fold(parts, op):
    parts = list(parts)
    while len(parts) > 1:
        parts = [op(a, b) for a, b in zip(parts[::2], parts[1::2])]
    return parts[0]


def lane_groups(width):
    return [slice(k, k + LANES) for k in range(0, width, LANES)]


def as_row(column_sums):
    return jnp.sum(column_sums.T, axis=0, keepdims=True)


def as_column(row):
    return jnp.broadcast_to(row, (LANES, row.shape[1])).T


def block(i):
    return pl.ds(pl.multiple_of(i * ROWS, ROWS), ROWS)


def stats_kernel(x_hbm, out_ref, x_ref, sems):
    cells, spots = x_ref.shape
    steps = cells // ROWS
    groups = lane_groups(spots)

    def copy(i):
        return pltpu.make_async_copy(x_hbm.at[block(i), :], x_ref.at[block(i), :], sems.at[i])

    for i in range(steps):
        copy(i).start()

    @pl.loop(0, steps)
    def _(i):
        copy(i).wait()
        rows = block(i)
        top = fold([x_ref[rows, g] for g in groups], jnp.maximum).astype(jnp.float32)
        total = fold([jnp.exp(x_ref[rows, g].astype(jnp.float32) - top) for g in groups], jnp.add)
        top, total = top.T, total.T
        row_top = jnp.max(top, axis=0, keepdims=True)
        row_total = jnp.sum(total * jnp.exp(top - row_top), axis=0, keepdims=True)
        out_ref[pl.ds(i, 1), :] = row_top + jnp.log(row_total)


def transpose_kernel(e_ref, out_ref):
    @pl.loop(0, e_ref.shape[0] // ROWS)
    def _(i):
        out_ref[:, block(i)] = e_ref[block(i), :].T


def forward_kernel(tile, x_ref, et_ref, log_ref, part_ref, low, column):
    cells, spots = x_ref.shape

    @pl.loop(0, cells // ROWS)
    def _(i):
        column[block(i), :] = as_column(log_ref[pl.ds(i, 1), :])

    tiles = [slice(k, k + tile) for k in range(0, spots, tile)]

    def fill(cols):
        for k in range(cols.start, cols.stop, LANES):
            g = slice(k, k + LANES)
            probs = jnp.exp(x_ref[:, g].astype(jnp.float32) - column[...])
            low[:, g] = probs.astype(jnp.bfloat16)

    fill(tiles[0])
    for cols, later in zip(tiles, tiles[1:] + [None]):
        part = jnp.dot(et_ref[...], low[:, cols], preferred_element_type=jnp.float32)
        part_ref[:, cols] = part.astype(jnp.bfloat16)
        if later is not None:
            fill(later)


def backward_kernel(size, x_ref, e_ref, d_ref, log_ref, probs_ref, dprobs_ref, dot_ref):
    cells, spots = probs_ref.shape

    def fill(first):
        for k in range(first, first + size, ROWS):
            rows = slice(k, k + ROWS)
            log_total = as_column(log_ref[k // ROWS : k // ROWS + 1, :])
            for g in lane_groups(spots):
                probs_ref[rows, g] = jnp.exp(x_ref[rows, g].astype(jnp.float32) - log_total)

    def row_dots(first):
        for k in range(first, first + size, ROWS):
            rows = slice(k, k + ROWS)
            parts = [probs_ref[rows, g] * dprobs_ref[rows, g] for g in lane_groups(spots)]
            dot_ref[k // ROWS : k // ROWS + 1, :] = as_row(fold(parts, jnp.add))

    for first in range(0, cells, size):
        rows = slice(first, first + size)
        dprobs_ref[rows, :] = jnp.dot(e_ref[rows, :], d_ref[...], preferred_element_type=jnp.float32)
        fill(first)
        if first:
            row_dots(first - size)
    row_dots(cells - size)


def gradient_kernel(scale, size, probs_ref, dprobs_ref, dot_ref, out_hbm, buf, sems):
    cells, spots = probs_ref.shape
    steps = cells // size
    inner = size // ROWS

    def copy(i):
        rows = pl.ds(pl.multiple_of(i * size, size), size)
        return pltpu.make_async_copy(buf.at[rows, :], out_hbm.at[rows, :], sems.at[i])

    @pl.loop(0, steps)
    def _(i):
        for h in range(inner):
            rows = block(i * inner + h)
            row_dot = as_column(dot_ref[pl.ds(i * inner + h, 1), :])
            for g in lane_groups(spots):
                grad = scale * probs_ref[rows, g] * (dprobs_ref[rows, g] - row_dot)
                buf[rows, g] = grad.astype(jnp.bfloat16)
        copy(i).start()

    for i in range(steps):
        copy(i).wait()


VMEM = pl.BlockSpec(memory_space=pltpu.VMEM)
HBM = pl.BlockSpec(memory_space=pltpu.HBM)


def params(mib):
    return pltpu.CompilerParams(vmem_limit_bytes=mib * MIB)


def cost(flops, moved, transcendentals=0):
    return pl.CostEstimate(flops=flops, bytes_accessed=moved, transcendentals=transcendentals)


def local_log_sum(logits):
    cells, spots = logits.shape
    steps = cells // ROWS
    return pl.pallas_call(
        stats_kernel,
        in_specs=[HBM],
        out_specs=VMEM,
        out_shape=jax.ShapeDtypeStruct((steps, ROWS), jnp.float32),
        scratch_shapes=[
            pltpu.VMEM((cells, spots), logits.dtype),
            pltpu.SemaphoreType.DMA((steps,)),
        ],
        compiler_params=params(8),
        cost_estimate=cost(cells * spots * 6, cells * spots * 2, cells * spots),
        name="stats",
    )(logits)


def transposed(expression):
    cells, genes = expression.shape
    return pl.pallas_call(
        transpose_kernel,
        in_specs=[VMEM],
        out_specs=VMEM,
        out_shape=jax.ShapeDtypeStruct((genes, cells), expression.dtype),
        compiler_params=params(8),
        cost_estimate=cost(0, cells * genes * 4),
        name="transpose",
    )(expression)


def partial_predicted(logits, expression_t, log_total):
    cells, spots = logits.shape
    genes = expression_t.shape[0]
    return pl.pallas_call(
        functools.partial(forward_kernel, 256),
        in_specs=[VMEM] * 3,
        out_specs=VMEM,
        out_shape=jax.ShapeDtypeStruct((genes, spots), jnp.bfloat16),
        scratch_shapes=[
            pltpu.VMEM((cells, spots), jnp.bfloat16),
            pltpu.VMEM((cells, LANES), jnp.float32),
        ],
        compiler_params=params(16),
        cost_estimate=cost(2 * cells * spots * genes, cells * spots * 4, cells * spots),
        name="forward",
    )(logits, expression_t, log_total)


def backward(logits, expression, d_pred, log_total):
    cells, spots = logits.shape
    genes = expression.shape[1]
    return pl.pallas_call(
        functools.partial(backward_kernel, 512),
        in_specs=[VMEM] * 4,
        out_specs=[VMEM] * 3,
        out_shape=[
            jax.ShapeDtypeStruct((cells, spots), jnp.float32),
            jax.ShapeDtypeStruct((cells, spots), jnp.float32),
            jax.ShapeDtypeStruct((cells // ROWS, ROWS), jnp.float32),
        ],
        compiler_params=params(12),
        cost_estimate=cost(2 * cells * spots * genes, cells * spots * 4, cells * spots),
        name="backward",
    )(logits, expression, d_pred, log_total)


def gradient(probs, d_probs, row_dot, scale):
    cells, spots = probs.shape
    size = 512
    return pl.pallas_call(
        functools.partial(gradient_kernel, scale, size),
        in_specs=[VMEM] * 3,
        out_specs=HBM,
        out_shape=jax.ShapeDtypeStruct((cells, spots), jnp.bfloat16),
        scratch_shapes=[
            pltpu.VMEM((cells, spots), jnp.bfloat16),
            pltpu.SemaphoreType.DMA((cells // size,)),
        ],
        compiler_params=params(12),
        cost_estimate=cost(cells * spots * 3, cells * spots * 4),
        name="gradient",
    )(probs, d_probs, row_dot)


def body(logits, expression, measured):
    spots = logits.shape[1]
    local_log = local_log_sum(pltpu.with_memory_space_constraint(logits, pltpu.HBM))
    expression_t = transposed(expression)
    log_total = narrow_combine(local_log, log_add)
    part = partial_predicted(logits, expression_t, log_total)
    part = part.reshape(Y, Z, X, R, spots)
    part = by_core(
        part.transpose(0, 2, 1, 3, 4).reshape(8, Z * R, spots),
        part.transpose(1, 0, 2, 3, 4).reshape(8, Y * X * R, spots),
    )
    part = swap(part, WIDE_STAGE).astype(jnp.float32).sum(0).astype(jnp.bfloat16)
    part = swap(part.reshape(8, R, spots), SHORT_STAGE)
    predicted = part.astype(jnp.float32).sum(0)
    sums = jnp.stack(
        [
            jnp.sum(predicted * measured, axis=1),
            jnp.sum(predicted * predicted, axis=1),
            jnp.sum(measured * measured, axis=1),
        ]
    )
    sums = narrow_combine(sums, jnp.add)
    inner, pred_sq, meas_sq = sums[0], sums[1], sums[2]
    inv_p = lax.rsqrt(pred_sq + 1e-06)
    inv_m = lax.rsqrt(meas_sq + 1e-06)
    similarity = inner * (inv_p * inv_m)
    share = (
        (similarity * inv_p * inv_p)[:, None] * predicted - (inv_p * inv_m)[:, None] * measured
    ).astype(jnp.bfloat16)
    share = swap(jnp.broadcast_to(share[None], (8, R, spots)), SHORT_STAGE).reshape(8 * R, spots)
    share = swap(jnp.broadcast_to(share[None], (8, 8 * R, spots)), WIDE_STAGE)
    d_pred = by_core(
        share.reshape(Y, X, Z, R, spots).transpose(0, 2, 1, 3, 4),
        share.reshape(Z, Y, X, R, spots).transpose(1, 0, 2, 3, 4),
    ).reshape(Y * Z * X * R, spots)
    probs, d_probs, row_dot = backward(logits, expression, d_pred, log_total)
    row_dot = narrow_combine(row_dot, jnp.add)
    grad = gradient(probs, d_probs, row_dot, float(spots * lax.axis_size("narrow")))
    return (grad, similarity)


def solution(mesh):
    placed = (P("wide", "narrow"), P("wide", None), P("wide", "narrow"))
    return jax.shard_map(
        body,
        mesh=mesh,
        in_specs=placed,
        out_specs=(P("wide", "narrow"), P("wide")),
        check_vma=False,
    )
```

```python
import functools

import jax
import jax.numpy as jnp
from jax import lax
from jax.experimental import pallas as pl
from jax.experimental.pallas import tpu as pltpu
from jax.sharding import PartitionSpec as P

Y, Z, X, R, N = 4, 8, 2, 8, 4
LANES = 128
ROWS = 256
MIB = 1 << 20


def wide_index(y, z, x):
    return (y * Z + z) * X + x


def device_index(y, z, x, n):
    return wide_index(y, z, x) * N + n


def yx_groups(n):
    return [[device_index(y, z, x, n) for y in range(Y) for x in range(X)] for z in range(Z)]


def z_groups(n):
    return [[device_index(y, z, x, n) for z in range(Z)] for y in range(Y) for x in range(X)]


WIDE_STAGE = [g for n in range(N) for g in (z_groups(n) if n % 2 else yx_groups(n))]
SHORT_STAGE = [g for n in range(N) for g in (yx_groups(n) if n % 2 else z_groups(n))]


def swap(v, groups):
    return lax.all_to_all(v, ("wide", "narrow"), 0, 0, axis_index_groups=groups)


def by_core(even, odd):
    return jnp.where(lax.axis_index("narrow") % 2 == 0, even, odd)


def narrow_combine(v, op):
    for d in (1, 2):
        v = op(v, lax.ppermute(v, "narrow", [(i, i ^ d) for i in range(4)]))
    return v


def log_add(a, b):
    top = jnp.maximum(a, b)
    return top + jnp.log(jnp.exp(a - top) + jnp.exp(b - top))


def fold(parts, op):
    parts = list(parts)
    while len(parts) > 1:
        parts = [op(a, b) for a, b in zip(parts[::2], parts[1::2])]
    return parts[0]


def lane_groups(width):
    return [slice(k, k + LANES) for k in range(0, width, LANES)]


def as_row(column_sums):
    return jnp.sum(column_sums.T, axis=0, keepdims=True)


def as_column(row):
    return jnp.broadcast_to(row, (LANES, row.shape[1])).T


def block(i):
    return pl.ds(pl.multiple_of(i * ROWS, ROWS), ROWS)


def stats_kernel(x_hbm, out_ref, x_ref, sems):
    cells, spots = x_ref.shape
    steps = cells // ROWS
    groups = lane_groups(spots)

    def copy(i):
        return pltpu.make_async_copy(x_hbm.at[block(i), :], x_ref.at[block(i), :], sems.at[i])

    for i in range(steps):
        copy(i).start()

    @pl.loop(0, steps)
    def _(i):
        copy(i).wait()
        rows = block(i)
        top = fold([x_ref[rows, g] for g in groups], jnp.maximum).astype(jnp.float32)
        total = fold([jnp.exp(x_ref[rows, g].astype(jnp.float32) - top) for g in groups], jnp.add)
        top, total = top.T, total.T
        row_top = jnp.max(top, axis=0, keepdims=True)
        row_total = jnp.sum(total * jnp.exp(top - row_top), axis=0, keepdims=True)
        out_ref[pl.ds(i, 1), :] = row_top + jnp.log(row_total)


def transpose_kernel(e_hbm, out_ref, e_ref, sems):
    steps = e_ref.shape[0] // ROWS

    def copy(i):
        return pltpu.make_async_copy(e_hbm.at[block(i), :], e_ref.at[block(i), :], sems.at[i])

    for i in range(steps):
        copy(i).start()

    @pl.loop(0, steps)
    def _(i):
        copy(i).wait()
        out_ref[:, block(i)] = e_ref[block(i), :].T


def forward_kernel(tile, x_ref, et_ref, log_ref, part_ref, low, column):
    cells, spots = x_ref.shape

    @pl.loop(0, cells // ROWS)
    def _(i):
        column[block(i), :] = as_column(log_ref[pl.ds(i, 1), :])

    tiles = [slice(k, k + tile) for k in range(0, spots, tile)]

    def fill(cols):
        for k in range(cols.start, cols.stop, LANES):
            g = slice(k, k + LANES)
            probs = jnp.exp(x_ref[:, g].astype(jnp.float32) - column[...])
            low[:, g] = probs.astype(jnp.bfloat16)

    fill(tiles[0])
    for cols, later in zip(tiles, tiles[1:] + [None]):
        part = jnp.dot(et_ref[...], low[:, cols], preferred_element_type=jnp.float32)
        part_ref[:, cols] = part.astype(jnp.bfloat16)
        if later is not None:
            fill(later)


def backward_kernel(size, x_ref, e_ref, d_ref, log_ref, probs_ref, dprobs_ref, dot_ref):
    cells, spots = probs_ref.shape

    def fill(first):
        for k in range(first, first + size, ROWS):
            rows = slice(k, k + ROWS)
            log_total = as_column(log_ref[k // ROWS : k // ROWS + 1, :])
            for g in lane_groups(spots):
                probs_ref[rows, g] = jnp.exp(x_ref[rows, g].astype(jnp.float32) - log_total)

    def row_dots(first):
        for k in range(first, first + size, ROWS):
            rows = slice(k, k + ROWS)
            parts = [probs_ref[rows, g] * dprobs_ref[rows, g] for g in lane_groups(spots)]
            dot_ref[k // ROWS : k // ROWS + 1, :] = as_row(fold(parts, jnp.add))

    for first in range(0, cells, size):
        rows = slice(first, first + size)
        dprobs_ref[rows, :] = jnp.dot(e_ref[rows, :], d_ref[...], preferred_element_type=jnp.float32)
        fill(first)
        if first:
            row_dots(first - size)
    row_dots(cells - size)


def gradient_kernel(scale, size, probs_ref, dprobs_ref, dot_ref, out_hbm, buf, sems):
    cells, spots = probs_ref.shape
    steps = cells // size
    inner = size // ROWS

    def copy(i):
        rows = pl.ds(pl.multiple_of(i * size, size), size)
        return pltpu.make_async_copy(buf.at[rows, :], out_hbm.at[rows, :], sems.at[i])

    @pl.loop(0, steps)
    def _(i):
        for h in range(inner):
            rows = block(i * inner + h)
            row_dot = as_column(dot_ref[pl.ds(i * inner + h, 1), :])
            for g in lane_groups(spots):
                grad = scale * probs_ref[rows, g] * (dprobs_ref[rows, g] - row_dot)
                buf[rows, g] = grad.astype(jnp.bfloat16)
        copy(i).start()

    for i in range(steps):
        copy(i).wait()


def gene_sums_kernel(part_ref, measured_ref, predicted_ref, sums_ref):
    rows = part_ref.shape[0]
    pairs = [part_ref[k : k + 2 * R, :].astype(jnp.float32) for k in range(0, rows, 2 * R)]
    pairs = fold(pairs, jnp.add)
    predicted = pairs[:R] + pairs[R:]
    predicted_ref[...] = predicted
    measured = measured_ref[...]
    groups = lane_groups(predicted.shape[1])
    for k, v in enumerate([predicted * measured, predicted * predicted, measured * measured]):
        sums_ref[k * R : (k + 1) * R, :] = fold([v[:, g] for g in groups], jnp.add)


def share_kernel(sums_ref, predicted_ref, measured_ref, share_ref, cosine_ref):
    sums = jnp.sum(sums_ref[...], axis=1, keepdims=True)
    inner, pred_sq, meas_sq = sums[:R], sums[R : 2 * R], sums[2 * R :]
    inv_p = lax.rsqrt(pred_sq + 1e-06)
    inv_m = lax.rsqrt(meas_sq + 1e-06)
    cosine = inner * (inv_p * inv_m)
    cosine_ref[...] = jnp.broadcast_to(cosine, cosine_ref.shape)
    share = cosine * inv_p * inv_p * predicted_ref[...] - inv_p * inv_m * measured_ref[...]
    share = jnp.concatenate([share, share]).astype(jnp.bfloat16)
    for k in range(0, share_ref.shape[0], 2 * R):
        share_ref[k : k + 2 * R, :] = share


VMEM = pl.BlockSpec(memory_space=pltpu.VMEM)
HBM = pl.BlockSpec(memory_space=pltpu.HBM)


def params(mib):
    return pltpu.CompilerParams(vmem_limit_bytes=mib * MIB)


def cost(flops, moved, transcendentals=0):
    return pl.CostEstimate(flops=flops, bytes_accessed=moved, transcendentals=transcendentals)


def local_log_sum(logits):
    cells, spots = logits.shape
    steps = cells // ROWS
    return pl.pallas_call(
        stats_kernel,
        in_specs=[HBM],
        out_specs=VMEM,
        out_shape=jax.ShapeDtypeStruct((steps, ROWS), jnp.float32),
        scratch_shapes=[
            pltpu.VMEM((cells, spots), logits.dtype),
            pltpu.SemaphoreType.DMA((steps,)),
        ],
        compiler_params=params(8),
        cost_estimate=cost(cells * spots * 6, cells * spots * 2, cells * spots),
        name="stats",
    )(logits)


def transposed(expression):
    cells, genes = expression.shape
    return pl.pallas_call(
        transpose_kernel,
        in_specs=[HBM],
        out_specs=VMEM,
        out_shape=jax.ShapeDtypeStruct((genes, cells), expression.dtype),
        scratch_shapes=[
            pltpu.VMEM((cells, genes), expression.dtype),
            pltpu.SemaphoreType.DMA((cells // ROWS,)),
        ],
        compiler_params=params(8),
        cost_estimate=cost(0, cells * genes * 4),
        name="transpose",
    )(expression)


def partial_predicted(logits, expression_t, log_total):
    cells, spots = logits.shape
    genes = expression_t.shape[0]
    return pl.pallas_call(
        functools.partial(forward_kernel, 256),
        in_specs=[VMEM] * 3,
        out_specs=VMEM,
        out_shape=jax.ShapeDtypeStruct((genes, spots), jnp.bfloat16),
        scratch_shapes=[
            pltpu.VMEM((cells, spots), jnp.bfloat16),
            pltpu.VMEM((cells, LANES), jnp.float32),
        ],
        compiler_params=params(16),
        cost_estimate=cost(2 * cells * spots * genes, cells * spots * 4, cells * spots),
        name="forward",
    )(logits, expression_t, log_total)


def backward(logits, expression, d_pred, log_total):
    cells, spots = logits.shape
    genes = expression.shape[1]
    return pl.pallas_call(
        functools.partial(backward_kernel, 512),
        in_specs=[VMEM] * 4,
        out_specs=[VMEM] * 3,
        out_shape=[
            jax.ShapeDtypeStruct((cells, spots), jnp.float32),
            jax.ShapeDtypeStruct((cells, spots), jnp.float32),
            jax.ShapeDtypeStruct((cells // ROWS, ROWS), jnp.float32),
        ],
        compiler_params=params(12),
        cost_estimate=cost(2 * cells * spots * genes, cells * spots * 4, cells * spots),
        name="backward",
    )(logits, expression, d_pred, log_total)


def gradient(probs, d_probs, row_dot, scale):
    cells, spots = probs.shape
    size = 512
    return pl.pallas_call(
        functools.partial(gradient_kernel, scale, size),
        in_specs=[VMEM] * 3,
        out_specs=HBM,
        out_shape=jax.ShapeDtypeStruct((cells, spots), jnp.bfloat16),
        scratch_shapes=[
            pltpu.VMEM((cells, spots), jnp.bfloat16),
            pltpu.SemaphoreType.DMA((cells // size,)),
        ],
        compiler_params=params(12),
        cost_estimate=cost(cells * spots * 3, cells * spots * 4),
        name="gradient",
    )(probs, d_probs, row_dot)


def gene_sums(part, measured):
    rows, spots = part.shape
    return pl.pallas_call(
        gene_sums_kernel,
        in_specs=[VMEM] * 2,
        out_specs=[VMEM] * 2,
        out_shape=[
            jax.ShapeDtypeStruct((R, spots), jnp.float32),
            jax.ShapeDtypeStruct((3 * R, LANES), jnp.float32),
        ],
        compiler_params=params(4),
        name="gene_sums",
    )(part, measured)


def gradient_share(sums, predicted, measured):
    spots = predicted.shape[1]
    return pl.pallas_call(
        share_kernel,
        in_specs=[VMEM] * 3,
        out_specs=[VMEM] * 2,
        out_shape=[
            jax.ShapeDtypeStruct((8 * R, spots), jnp.bfloat16),
            jax.ShapeDtypeStruct((R, LANES), jnp.float32),
        ],
        compiler_params=params(4),
        name="share",
    )(sums, predicted, measured)


def body(logits, expression, measured):
    spots = logits.shape[1]
    local_log = local_log_sum(pltpu.with_memory_space_constraint(logits, pltpu.HBM))
    expression_t = transposed(pltpu.with_memory_space_constraint(expression, pltpu.HBM))
    log_total = narrow_combine(local_log, log_add)
    part = partial_predicted(logits, expression_t, log_total)
    part = part.reshape(Y, Z, X, R, spots)
    part = by_core(
        part.transpose(0, 2, 1, 3, 4).reshape(8, Z * R, spots),
        part.transpose(1, 0, 2, 3, 4).reshape(8, Y * X * R, spots),
    )
    part = swap(part, WIDE_STAGE).astype(jnp.float32).sum(0).astype(jnp.bfloat16)
    part = swap(part.reshape(8, R, spots), SHORT_STAGE).reshape(8 * R, spots)
    predicted, sums = gene_sums(part, measured)
    share, cosine = gradient_share(narrow_combine(sums, jnp.add), predicted, measured)
    similarity = cosine[:, 0]
    share = swap(share.reshape(8, R, spots), SHORT_STAGE).reshape(8 * R, spots)
    share = swap(jnp.broadcast_to(share[None], (8, 8 * R, spots)), WIDE_STAGE)
    d_pred = by_core(
        share.reshape(Y, X, Z, R, spots).transpose(0, 2, 1, 3, 4),
        share.reshape(Z, Y, X, R, spots).transpose(1, 0, 2, 3, 4),
    ).reshape(Y * Z * X * R, spots)
    probs, d_probs, row_dot = backward(logits, expression, d_pred, log_total)
    row_dot = narrow_combine(row_dot, jnp.add)
    grad = gradient(probs, d_probs, row_dot, float(spots * lax.axis_size("narrow")))
    return (grad, similarity)


def solution(mesh):
    placed = (P("wide", "narrow"), P("wide", None), P("wide", "narrow"))
    return jax.shard_map(
        body,
        mesh=mesh,
        in_specs=placed,
        out_specs=(P("wide", "narrow"), P("wide")),
        check_vma=False,
    )
```

```python
import functools

import jax
import jax.numpy as jnp
from jax import lax
from jax.experimental import pallas as pl
from jax.experimental.pallas import tpu as pltpu
from jax.sharding import PartitionSpec as P

Y, Z, X, R, N = 4, 8, 2, 8, 4
H, L = 4, 2
FOUR, MEMBERS = 4, 16
LANES = 128
ROWS = 256
FORWARD_TILE = 256
MIB = 1 << 20


def wide_index(y, z, x):
    return (y * Z + z) * X + x


def device_index(y, z, x, n):
    return wide_index(y, z, x) * N + n


def zx_groups(n):
    return [[device_index(y, z, x, n) for z in range(Z) for x in range(X)] for y in range(Y)]


def yh_groups(n):
    return [
        [device_index(y, 2 * h + l, x, n) for y in range(Y) for h in range(H)]
        for x in range(X)
        for l in range(L)
    ]


def partner(y, z, x, n, k):
    if n % 2 == 0:
        return device_index((y + k) % Y, z, x, n)
    o = (L * x + z % L) ^ k
    return device_index(y, z - z % L + o % L, o // L, n)


FIRST = {
    k: [
        (device_index(y, z, x, n), partner(y, z, x, n, k))
        for y in range(Y)
        for z in range(Z)
        for x in range(X)
        for n in range(N)
    ]
    for k in (1, 2, 3)
}
SECOND = [g for n in range(N) for g in (yh_groups(n) if n % 2 else zx_groups(n))]
ORDER = (2, 1, 3)


def send_first(v, k):
    return lax.ppermute(v, ("wide", "narrow"), FIRST[k])


def swap_second(v):
    return lax.all_to_all(v, ("wide", "narrow"), 0, 0, axis_index_groups=SECOND)


def by_core(even, odd):
    return jnp.where(lax.axis_index("narrow") % 2 == 0, even, odd)


def own_block():
    wide = lax.axis_index("wide")
    return by_core(wide // (Z * X), (wide % X) * L + (wide // X) % L)


def reduce_scatter(part):
    spots = part.shape[1]
    blocks = by_core(
        part.reshape(FOUR, -1, spots),
        part.reshape(Y, H, L, X, R, spots)
        .transpose(3, 2, 0, 1, 4, 5)
        .reshape(FOUR, -1, spots),
    )
    own = own_block()

    def pick(i):
        return lax.dynamic_index_in_dim(blocks, i, 0, keepdims=False)

    got = [send_first(pick(by_core((own + k) % FOUR, own ^ k)), k) for k in ORDER]
    total = fold([v.astype(jnp.float32) for v in [pick(own)] + got], jnp.add)
    total = total.astype(jnp.bfloat16).reshape(MEMBERS, R, spots)
    return swap_second(total).reshape(MEMBERS * R, spots)


def all_gather_second(share):
    spots = share.shape[1]
    return swap_second(share.reshape(MEMBERS, R, spots)).reshape(MEMBERS * R, spots)


def all_gather_first(block):
    spots = block.shape[1]
    got = {k: send_first(block, k) for k in ORDER}
    got[0] = block
    own = own_block()
    blocks = jnp.stack(
        [
            lax.select_n(by_core((own - j) % FOUR, own ^ j), *[got[k] for k in range(FOUR)])
            for j in range(FOUR)
        ]
    )
    return by_core(
        blocks.reshape(-1, spots),
        blocks.reshape(X, L, Y, H, R, spots).transpose(2, 3, 1, 0, 4, 5).reshape(-1, spots),
    )


def narrow_combine(v, op):
    for d in (1, 2):
        v = op(v, lax.ppermute(v, "narrow", [(i, i ^ d) for i in range(4)]))
    return v


def log_add(a, b):
    top = jnp.maximum(a, b)
    return top + jnp.log(jnp.exp(a - top) + jnp.exp(b - top))


def fold(parts, op):
    parts = list(parts)
    while len(parts) > 1:
        parts = [op(a, b) for a, b in zip(parts[::2], parts[1::2])]
    return parts[0]


def lane_groups(width):
    return [slice(k, k + LANES) for k in range(0, width, LANES)]


def as_row(column_sums):
    return jnp.sum(column_sums.T, axis=0, keepdims=True)


def as_column(row):
    return jnp.broadcast_to(row, (LANES, row.shape[1])).T


def block(i):
    return pl.ds(pl.multiple_of(i * ROWS, ROWS), ROWS)


def stats_kernel(x_hbm, out_ref, x_ref, sems):
    cells, spots = x_ref.shape
    steps = cells // ROWS
    groups = lane_groups(spots)

    def copy(i):
        return pltpu.make_async_copy(x_hbm.at[block(i), :], x_ref.at[block(i), :], sems.at[i])

    for i in range(steps):
        copy(i).start()

    @pl.loop(0, steps)
    def _(i):
        copy(i).wait()
        rows = block(i)
        top = fold([x_ref[rows, g] for g in groups], jnp.maximum).astype(jnp.float32)
        total = fold([jnp.exp(x_ref[rows, g].astype(jnp.float32) - top) for g in groups], jnp.add)
        top, total = top.T, total.T
        row_top = jnp.max(top, axis=0, keepdims=True)
        row_total = jnp.sum(total * jnp.exp(top - row_top), axis=0, keepdims=True)
        out_ref[pl.ds(i, 1), :] = row_top + jnp.log(row_total)


def transpose_kernel(e_hbm, out_ref, e_ref, sems):
    steps = e_ref.shape[0] // ROWS

    def copy(i):
        return pltpu.make_async_copy(e_hbm.at[block(i), :], e_ref.at[block(i), :], sems.at[i])

    for i in range(steps):
        copy(i).start()

    @pl.loop(0, steps)
    def _(i):
        copy(i).wait()
        out_ref[:, block(i)] = e_ref[block(i), :].T


def probs_kernel(x_hbm, e_hbm, log_ref, probs_ref, e_ref, x_ref, sems):
    cells, spots = x_ref.shape
    steps = cells // ROWS

    def copy(i):
        return pltpu.make_async_copy(x_hbm.at[block(i), :], x_ref.at[block(i), :], sems.at[i])

    for i in range(steps):
        copy(i).start()
    expression = pltpu.make_async_copy(e_hbm, e_ref, sems.at[steps])
    expression.start()

    @pl.loop(0, steps)
    def _(i):
        copy(i).wait()
        log_total = as_column(log_ref[pl.ds(i, 1), :])
        for g in lane_groups(spots):
            probs_ref[block(i), g] = jnp.exp(x_ref[block(i), g].astype(jnp.float32) - log_total)

    expression.wait()


def forward_kernel(tile, x_hbm, et_ref, log_ref, part_ref, x_ref, low, column, sems):
    cells, spots = x_ref.shape
    tiles = [slice(k, k + tile) for k in range(0, spots, tile)]
    copies = [
        pltpu.make_async_copy(x_hbm.at[:, cols], x_ref.at[:, cols], sems.at[k])
        for k, cols in enumerate(tiles)
    ]
    for copy in copies:
        copy.start()

    @pl.loop(0, cells // ROWS)
    def _(i):
        column[block(i), :] = as_column(log_ref[pl.ds(i, 1), :])

    def fill(cols):
        copies[cols.start // tile].wait()
        for k in range(cols.start, cols.stop, LANES):
            g = slice(k, k + LANES)
            probs = jnp.exp(x_ref[:, g].astype(jnp.float32) - column[...])
            low[:, g] = probs.astype(jnp.bfloat16)

    fill(tiles[0])
    for cols, later in zip(tiles, tiles[1:] + [None]):
        part = jnp.dot(et_ref[...], low[:, cols], preferred_element_type=jnp.float32)
        part_ref[:, cols] = part.astype(jnp.bfloat16)
        if later is not None:
            fill(later)


def backward_kernel(size, probs_ref, e_ref, d_ref, dprobs_ref, dot_ref):
    cells, spots = probs_ref.shape

    def row_dots(first):
        for k in range(first, first + size, ROWS):
            rows = slice(k, k + ROWS)
            parts = [probs_ref[rows, g] * dprobs_ref[rows, g] for g in lane_groups(spots)]
            dot_ref[k // ROWS : k // ROWS + 1, :] = as_row(fold(parts, jnp.add))

    for first in range(0, cells, size):
        rows = slice(first, first + size)
        dprobs_ref[rows, :] = jnp.dot(e_ref[rows, :], d_ref[...], preferred_element_type=jnp.float32)
        if first:
            row_dots(first - size)
    row_dots(cells - size)


def gradient_kernel(scale, size, probs_ref, dprobs_ref, dot_ref, out_hbm, buf, sems):
    cells, spots = probs_ref.shape
    steps = cells // size
    inner = size // ROWS

    def copy(i):
        rows = pl.ds(pl.multiple_of(i * size, size), size)
        return pltpu.make_async_copy(buf.at[rows, :], out_hbm.at[rows, :], sems.at[i])

    @pl.loop(0, steps)
    def _(i):
        for h in range(inner):
            rows = block(i * inner + h)
            row_dot = as_column(dot_ref[pl.ds(i * inner + h, 1), :])
            for g in lane_groups(spots):
                grad = scale * probs_ref[rows, g] * (dprobs_ref[rows, g] - row_dot)
                buf[rows, g] = grad.astype(jnp.bfloat16)
        copy(i).start()

    for i in range(steps):
        copy(i).wait()


def gene_sums_kernel(part_ref, measured_ref, predicted_ref, sums_ref):
    rows = part_ref.shape[0]
    pairs = [part_ref[k : k + 2 * R, :].astype(jnp.float32) for k in range(0, rows, 2 * R)]
    pairs = fold(pairs, jnp.add)
    predicted = pairs[:R] + pairs[R:]
    predicted_ref[...] = predicted
    measured = measured_ref[...]
    groups = lane_groups(predicted.shape[1])
    for k, v in enumerate([predicted * measured, predicted * predicted, measured * measured]):
        sums_ref[k * R : (k + 1) * R, :] = fold([v[:, g] for g in groups], jnp.add)


def share_kernel(sums_ref, predicted_ref, measured_ref, share_ref, cosine_ref):
    sums = jnp.sum(sums_ref[...], axis=1, keepdims=True)
    inner, pred_sq, meas_sq = sums[:R], sums[R : 2 * R], sums[2 * R :]
    inv_p = lax.rsqrt(pred_sq + 1e-06)
    inv_m = lax.rsqrt(meas_sq + 1e-06)
    cosine = inner * (inv_p * inv_m)
    cosine_ref[...] = jnp.broadcast_to(cosine, cosine_ref.shape)
    share = cosine * inv_p * inv_p * predicted_ref[...] - inv_p * inv_m * measured_ref[...]
    share = jnp.concatenate([share, share]).astype(jnp.bfloat16)
    for k in range(0, share_ref.shape[0], 2 * R):
        share_ref[k : k + 2 * R, :] = share


VMEM = pl.BlockSpec(memory_space=pltpu.VMEM)
HBM = pl.BlockSpec(memory_space=pltpu.HBM)


def params(mib):
    return pltpu.CompilerParams(vmem_limit_bytes=mib * MIB)


def cost(flops, moved, transcendentals=0):
    return pl.CostEstimate(flops=flops, bytes_accessed=moved, transcendentals=transcendentals)


def local_log_sum(logits):
    cells, spots = logits.shape
    steps = cells // ROWS
    return pl.pallas_call(
        stats_kernel,
        in_specs=[HBM],
        out_specs=VMEM,
        out_shape=jax.ShapeDtypeStruct((steps, ROWS), jnp.float32),
        scratch_shapes=[
            pltpu.VMEM((cells, spots), logits.dtype),
            pltpu.SemaphoreType.DMA((steps,)),
        ],
        compiler_params=params(8),
        cost_estimate=cost(cells * spots * 6, cells * spots * 2, cells * spots),
        name="stats",
    )(logits)


def transposed(expression):
    cells, genes = expression.shape
    return pl.pallas_call(
        transpose_kernel,
        in_specs=[HBM],
        out_specs=VMEM,
        out_shape=jax.ShapeDtypeStruct((genes, cells), expression.dtype),
        scratch_shapes=[
            pltpu.VMEM((cells, genes), expression.dtype),
            pltpu.SemaphoreType.DMA((cells // ROWS,)),
        ],
        compiler_params=params(8),
        cost_estimate=cost(0, cells * genes * 4),
        name="transpose",
    )(expression)


def probabilities(logits, expression, log_total):
    cells, spots = logits.shape
    steps = cells // ROWS
    return pl.pallas_call(
        probs_kernel,
        in_specs=[HBM, HBM, VMEM],
        out_specs=[VMEM, VMEM],
        out_shape=[
            jax.ShapeDtypeStruct((cells, spots), jnp.float32),
            jax.ShapeDtypeStruct(expression.shape, expression.dtype),
        ],
        scratch_shapes=[
            pltpu.VMEM((cells, spots), logits.dtype),
            pltpu.SemaphoreType.DMA((steps + 1,)),
        ],
        compiler_params=params(8),
        cost_estimate=cost(cells * spots * 4, cells * spots * 4, cells * spots),
        name="probs",
    )(logits, expression, log_total)


def partial_predicted(logits, expression_t, log_total):
    cells, spots = logits.shape
    genes = expression_t.shape[0]
    return pl.pallas_call(
        functools.partial(forward_kernel, FORWARD_TILE),
        in_specs=[HBM, VMEM, VMEM],
        out_specs=VMEM,
        out_shape=jax.ShapeDtypeStruct((genes, spots), jnp.bfloat16),
        scratch_shapes=[
            pltpu.VMEM((cells, spots), jnp.bfloat16),
            pltpu.VMEM((cells, spots), jnp.bfloat16),
            pltpu.VMEM((cells, LANES), jnp.float32),
            pltpu.SemaphoreType.DMA((spots // FORWARD_TILE,)),
        ],
        compiler_params=params(16),
        cost_estimate=cost(2 * cells * spots * genes, cells * spots * 4, cells * spots),
        name="forward",
    )(logits, expression_t, log_total)


def backward(probs, expression, d_pred):
    cells, spots = probs.shape
    genes = expression.shape[1]
    return pl.pallas_call(
        functools.partial(backward_kernel, 512),
        in_specs=[VMEM] * 3,
        out_specs=[VMEM] * 2,
        out_shape=[
            jax.ShapeDtypeStruct((cells, spots), jnp.float32),
            jax.ShapeDtypeStruct((cells // ROWS, ROWS), jnp.float32),
        ],
        compiler_params=params(8),
        cost_estimate=cost(2 * cells * spots * genes, cells * spots * 4),
        name="backward",
    )(probs, expression, d_pred)


def gradient(probs, d_probs, row_dot, scale):
    cells, spots = probs.shape
    size = 512
    return pl.pallas_call(
        functools.partial(gradient_kernel, scale, size),
        in_specs=[VMEM] * 3,
        out_specs=HBM,
        out_shape=jax.ShapeDtypeStruct((cells, spots), jnp.bfloat16),
        scratch_shapes=[
            pltpu.VMEM((cells, spots), jnp.bfloat16),
            pltpu.SemaphoreType.DMA((cells // size,)),
        ],
        compiler_params=params(12),
        cost_estimate=cost(cells * spots * 3, cells * spots * 4),
        name="gradient",
    )(probs, d_probs, row_dot)


def gene_sums(part, measured):
    rows, spots = part.shape
    return pl.pallas_call(
        gene_sums_kernel,
        in_specs=[VMEM] * 2,
        out_specs=[VMEM] * 2,
        out_shape=[
            jax.ShapeDtypeStruct((R, spots), jnp.float32),
            jax.ShapeDtypeStruct((3 * R, LANES), jnp.float32),
        ],
        compiler_params=params(4),
        name="gene_sums",
    )(part, measured)


def gradient_share(sums, predicted, measured):
    spots = predicted.shape[1]
    return pl.pallas_call(
        share_kernel,
        in_specs=[VMEM] * 3,
        out_specs=[VMEM] * 2,
        out_shape=[
            jax.ShapeDtypeStruct((MEMBERS * R, spots), jnp.bfloat16),
            jax.ShapeDtypeStruct((R, LANES), jnp.float32),
        ],
        compiler_params=params(4),
        name="share",
    )(sums, predicted, measured)


def body(logits, expression, measured):
    spots = logits.shape[1]
    far_logits = pltpu.with_memory_space_constraint(logits, pltpu.HBM)
    far_expression = pltpu.with_memory_space_constraint(expression, pltpu.HBM)
    local_log = local_log_sum(far_logits)
    expression_t = transposed(far_expression)
    log_total = narrow_combine(local_log, log_add)
    part = partial_predicted(far_logits, expression_t, log_total)
    part = reduce_scatter(part)
    predicted, sums = gene_sums(part, measured)
    share, cosine = gradient_share(narrow_combine(sums, jnp.add), predicted, measured)
    similarity = cosine[:, 0]
    share, log_total = lax.optimization_barrier((all_gather_second(share), log_total))
    probs, expression = probabilities(far_logits, far_expression, log_total)
    d_pred = all_gather_first(share)
    d_probs, row_dot = backward(probs, expression, d_pred)
    row_dot = narrow_combine(row_dot, jnp.add)
    grad = gradient(probs, d_probs, row_dot, float(spots * lax.axis_size("narrow")))
    return (grad, similarity)


def solution(mesh):
    placed = (P("wide", "narrow"), P("wide", None), P("wide", "narrow"))
    return jax.shard_map(
        body,
        mesh=mesh,
        in_specs=placed,
        out_specs=(P("wide", "narrow"), P("wide")),
        check_vma=False,
    )
```

```python
import functools

import jax
import jax.numpy as jnp
from jax import lax
from jax.experimental import pallas as pl
from jax.experimental.pallas import tpu as pltpu
from jax.sharding import PartitionSpec as P

Y, Z, X, R, N = 4, 8, 2, 8, 4
H, L = 4, 2
FOUR, MEMBERS = 4, 16
LANES = 128
ROWS = 256
MIB = 1 << 20


def wide_index(y, z, x):
    return (y * Z + z) * X + x


def device_index(y, z, x, n):
    return wide_index(y, z, x) * N + n


def zx_groups(n):
    return [[device_index(y, z, x, n) for z in range(Z) for x in range(X)] for y in range(Y)]


def yh_groups(n):
    return [
        [device_index(y, 2 * h + l, x, n) for y in range(Y) for h in range(H)]
        for x in range(X)
        for l in range(L)
    ]


def partner(y, z, x, n, k):
    if n % 2 == 0:
        return device_index((y + k) % Y, z, x, n)
    o = (L * x + z % L) ^ k
    return device_index(y, z - z % L + o % L, o // L, n)


FIRST = {
    k: [
        (device_index(y, z, x, n), partner(y, z, x, n, k))
        for y in range(Y)
        for z in range(Z)
        for x in range(X)
        for n in range(N)
    ]
    for k in (1, 2, 3)
}
SECOND = [g for n in range(N) for g in (yh_groups(n) if n % 2 else zx_groups(n))]
ORDER = (2, 1, 3)


def send_first(v, k):
    return lax.ppermute(v, ("wide", "narrow"), FIRST[k])


def swap_second(v):
    return lax.all_to_all(v, ("wide", "narrow"), 0, 0, axis_index_groups=SECOND)


def by_core(even, odd):
    return jnp.where(lax.axis_index("narrow") % 2 == 0, even, odd)


def own_block():
    wide = lax.axis_index("wide")
    return by_core(wide // (Z * X), (wide % X) * L + (wide // X) % L)


def reduce_scatter(part):
    spots = part.shape[1]
    blocks = by_core(
        part.reshape(FOUR, -1, spots),
        part.reshape(Y, H, L, X, R, spots)
        .transpose(3, 2, 0, 1, 4, 5)
        .reshape(FOUR, -1, spots),
    )
    own = own_block()

    def pick(i):
        return lax.dynamic_index_in_dim(blocks, i, 0, keepdims=False)

    got = [send_first(pick(by_core((own + k) % FOUR, own ^ k)), k) for k in ORDER]
    total = fold([v.astype(jnp.float32) for v in [pick(own)] + got], jnp.add)
    total = total.astype(jnp.bfloat16).reshape(MEMBERS, R, spots)
    return swap_second(total).reshape(MEMBERS * R, spots)


def all_gather_second(share):
    spots = share.shape[1]
    return swap_second(share.reshape(MEMBERS, R, spots)).reshape(MEMBERS * R, spots)


def all_gather_first(block):
    spots = block.shape[1]
    got = {k: send_first(block, k) for k in ORDER}
    got[0] = block
    own = own_block()
    blocks = jnp.stack(
        [
            lax.select_n(by_core((own - j) % FOUR, own ^ j), *[got[k] for k in range(FOUR)])
            for j in range(FOUR)
        ]
    )
    return by_core(
        blocks.reshape(-1, spots),
        blocks.reshape(X, L, Y, H, R, spots).transpose(2, 3, 1, 0, 4, 5).reshape(-1, spots),
    )


def narrow_combine(v, op):
    for d in (1, 2):
        v = op(v, lax.ppermute(v, "narrow", [(i, i ^ d) for i in range(4)]))
    return v


def log_add(a, b):
    top = jnp.maximum(a, b)
    return top + jnp.log(jnp.exp(a - top) + jnp.exp(b - top))


def fold(parts, op):
    parts = list(parts)
    while len(parts) > 1:
        parts = [op(a, b) for a, b in zip(parts[::2], parts[1::2])]
    return parts[0]


def lane_groups(width):
    return [slice(k, k + LANES) for k in range(0, width, LANES)]


def as_row(column_sums):
    return jnp.sum(column_sums.T, axis=0, keepdims=True)


def as_column(row):
    return jnp.broadcast_to(row, (LANES, row.shape[1])).T


def block(i):
    return pl.ds(pl.multiple_of(i * ROWS, ROWS), ROWS)


def stats_kernel(x_hbm, out_ref, x_ref, sems):
    cells, spots = x_ref.shape
    steps = cells // ROWS
    groups = lane_groups(spots)

    def copy(i):
        return pltpu.make_async_copy(x_hbm.at[block(i), :], x_ref.at[block(i), :], sems.at[i])

    for i in range(steps):
        copy(i).start()

    @pl.loop(0, steps)
    def _(i):
        copy(i).wait()
        rows = block(i)
        top = fold([x_ref[rows, g] for g in groups], jnp.maximum).astype(jnp.float32)
        total = fold([jnp.exp(x_ref[rows, g].astype(jnp.float32) - top) for g in groups], jnp.add)
        top, total = top.T, total.T
        row_top = jnp.max(top, axis=0, keepdims=True)
        row_total = jnp.sum(total * jnp.exp(top - row_top), axis=0, keepdims=True)
        out_ref[pl.ds(i, 1), :] = row_top + jnp.log(row_total)


def transpose_kernel(e_hbm, out_ref, e_ref, sems):
    steps = e_ref.shape[0] // ROWS

    def copy(i):
        return pltpu.make_async_copy(e_hbm.at[block(i), :], e_ref.at[block(i), :], sems.at[i])

    for i in range(steps):
        copy(i).start()

    @pl.loop(0, steps)
    def _(i):
        copy(i).wait()
        out_ref[:, block(i)] = e_ref[block(i), :].T


def probs_kernel(x_hbm, e_hbm, log_ref, probs_ref, e_ref, x_ref, sems):
    cells, spots = x_ref.shape
    steps = cells // ROWS

    def copy(i):
        return pltpu.make_async_copy(x_hbm.at[block(i), :], x_ref.at[block(i), :], sems.at[i])

    for i in range(steps):
        copy(i).start()
    expression = pltpu.make_async_copy(e_hbm, e_ref, sems.at[steps])
    expression.start()

    @pl.loop(0, steps)
    def _(i):
        copy(i).wait()
        log_total = as_column(log_ref[pl.ds(i, 1), :])
        for g in lane_groups(spots):
            probs_ref[block(i), g] = jnp.exp(x_ref[block(i), g].astype(jnp.float32) - log_total)

    expression.wait()


def forward_kernel(x_hbm, et_ref, log_ref, part_ref, x_ref, low, sems):
    cells, spots = x_ref.shape
    steps = cells // ROWS

    def copy(i):
        return pltpu.make_async_copy(x_hbm.at[block(i), :], x_ref.at[block(i), :], sems.at[i])

    for i in range(steps):
        copy(i).start()

    @pl.loop(0, steps)
    def _(i):
        copy(i).wait()
        log_total = as_column(log_ref[pl.ds(i, 1), :])
        for g in lane_groups(spots):
            probs = jnp.exp(x_ref[block(i), g].astype(jnp.float32) - log_total)
            low[block(i), g] = probs.astype(jnp.bfloat16)

    part = jnp.dot(et_ref[...], low[...], preferred_element_type=jnp.float32)
    part_ref[...] = part.astype(jnp.bfloat16)


def backward_kernel(size, probs_ref, e_ref, d_ref, dprobs_ref, dot_ref):
    cells, spots = probs_ref.shape

    def row_dots(first):
        for k in range(first, first + size, ROWS):
            rows = slice(k, k + ROWS)
            parts = [probs_ref[rows, g] * dprobs_ref[rows, g] for g in lane_groups(spots)]
            dot_ref[k // ROWS : k // ROWS + 1, :] = as_row(fold(parts, jnp.add))

    for first in range(0, cells, size):
        rows = slice(first, first + size)
        dprobs_ref[rows, :] = jnp.dot(e_ref[rows, :], d_ref[...], preferred_element_type=jnp.float32)
        if first:
            row_dots(first - size)
    row_dots(cells - size)


def gradient_kernel(scale, size, probs_ref, dprobs_ref, dot_ref, out_hbm, buf, sems):
    cells, spots = probs_ref.shape
    steps = cells // size
    inner = size // ROWS

    def copy(i):
        rows = pl.ds(pl.multiple_of(i * size, size), size)
        return pltpu.make_async_copy(buf.at[rows, :], out_hbm.at[rows, :], sems.at[i])

    @pl.loop(0, steps)
    def _(i):
        for h in range(inner):
            rows = block(i * inner + h)
            row_dot = as_column(dot_ref[pl.ds(i * inner + h, 1), :])
            for g in lane_groups(spots):
                grad = scale * probs_ref[rows, g] * (dprobs_ref[rows, g] - row_dot)
                buf[rows, g] = grad.astype(jnp.bfloat16)
        copy(i).start()

    for i in range(steps):
        copy(i).wait()


def gene_sums_kernel(part_ref, measured_ref, predicted_ref, sums_ref):
    rows = part_ref.shape[0]
    pairs = [part_ref[k : k + 2 * R, :].astype(jnp.float32) for k in range(0, rows, 2 * R)]
    pairs = fold(pairs, jnp.add)
    predicted = pairs[:R] + pairs[R:]
    predicted_ref[...] = predicted
    measured = measured_ref[...]
    groups = lane_groups(predicted.shape[1])
    for k, v in enumerate([predicted * measured, predicted * predicted, measured * measured]):
        sums_ref[k * R : (k + 1) * R, :] = fold([v[:, g] for g in groups], jnp.add)


def share_kernel(sums_ref, predicted_ref, measured_ref, share_ref, cosine_ref):
    sums = jnp.sum(sums_ref[...], axis=1, keepdims=True)
    inner, pred_sq, meas_sq = sums[:R], sums[R : 2 * R], sums[2 * R :]
    inv_p = lax.rsqrt(pred_sq + 1e-06)
    inv_m = lax.rsqrt(meas_sq + 1e-06)
    cosine = inner * (inv_p * inv_m)
    cosine_ref[...] = jnp.broadcast_to(cosine, cosine_ref.shape)
    share = cosine * inv_p * inv_p * predicted_ref[...] - inv_p * inv_m * measured_ref[...]
    share = jnp.concatenate([share, share]).astype(jnp.bfloat16)
    for k in range(0, share_ref.shape[0], 2 * R):
        share_ref[k : k + 2 * R, :] = share


VMEM = pl.BlockSpec(memory_space=pltpu.VMEM)
HBM = pl.BlockSpec(memory_space=pltpu.HBM)


def params(mib):
    return pltpu.CompilerParams(vmem_limit_bytes=mib * MIB)


def cost(flops, moved, transcendentals=0):
    return pl.CostEstimate(flops=flops, bytes_accessed=moved, transcendentals=transcendentals)


def local_log_sum(logits):
    cells, spots = logits.shape
    steps = cells // ROWS
    return pl.pallas_call(
        stats_kernel,
        in_specs=[HBM],
        out_specs=VMEM,
        out_shape=jax.ShapeDtypeStruct((steps, ROWS), jnp.float32),
        scratch_shapes=[
            pltpu.VMEM((cells, spots), logits.dtype),
            pltpu.SemaphoreType.DMA((steps,)),
        ],
        compiler_params=params(8),
        cost_estimate=cost(cells * spots * 6, cells * spots * 2, cells * spots),
        name="stats",
    )(logits)


def transposed(expression):
    cells, genes = expression.shape
    return pl.pallas_call(
        transpose_kernel,
        in_specs=[HBM],
        out_specs=VMEM,
        out_shape=jax.ShapeDtypeStruct((genes, cells), expression.dtype),
        scratch_shapes=[
            pltpu.VMEM((cells, genes), expression.dtype),
            pltpu.SemaphoreType.DMA((cells // ROWS,)),
        ],
        compiler_params=params(8),
        cost_estimate=cost(0, cells * genes * 4),
        name="transpose",
    )(expression)


def probabilities(logits, expression, log_total):
    cells, spots = logits.shape
    steps = cells // ROWS
    return pl.pallas_call(
        probs_kernel,
        in_specs=[HBM, HBM, VMEM],
        out_specs=[VMEM, VMEM],
        out_shape=[
            jax.ShapeDtypeStruct((cells, spots), jnp.float32),
            jax.ShapeDtypeStruct(expression.shape, expression.dtype),
        ],
        scratch_shapes=[
            pltpu.VMEM((cells, spots), logits.dtype),
            pltpu.SemaphoreType.DMA((steps + 1,)),
        ],
        compiler_params=params(8),
        cost_estimate=cost(cells * spots * 4, cells * spots * 4, cells * spots),
        name="probs",
    )(logits, expression, log_total)


def partial_predicted(logits, expression_t, log_total):
    cells, spots = logits.shape
    genes = expression_t.shape[0]
    return pl.pallas_call(
        forward_kernel,
        in_specs=[HBM, VMEM, VMEM],
        out_specs=VMEM,
        out_shape=jax.ShapeDtypeStruct((genes, spots), jnp.bfloat16),
        scratch_shapes=[
            pltpu.VMEM((cells, spots), jnp.bfloat16),
            pltpu.VMEM((cells, spots), jnp.bfloat16),
            pltpu.SemaphoreType.DMA((cells // ROWS,)),
        ],
        compiler_params=params(16),
        cost_estimate=cost(2 * cells * spots * genes, cells * spots * 4, cells * spots),
        name="forward",
    )(logits, expression_t, log_total)


def backward(probs, expression, d_pred):
    cells, spots = probs.shape
    genes = expression.shape[1]
    return pl.pallas_call(
        functools.partial(backward_kernel, 512),
        in_specs=[VMEM] * 3,
        out_specs=[VMEM] * 2,
        out_shape=[
            jax.ShapeDtypeStruct((cells, spots), jnp.float32),
            jax.ShapeDtypeStruct((cells // ROWS, ROWS), jnp.float32),
        ],
        compiler_params=params(8),
        cost_estimate=cost(2 * cells * spots * genes, cells * spots * 4),
        name="backward",
    )(probs, expression, d_pred)


def gradient(probs, d_probs, row_dot, scale):
    cells, spots = probs.shape
    size = 512
    return pl.pallas_call(
        functools.partial(gradient_kernel, scale, size),
        in_specs=[VMEM] * 3,
        out_specs=HBM,
        out_shape=jax.ShapeDtypeStruct((cells, spots), jnp.bfloat16),
        scratch_shapes=[
            pltpu.VMEM((cells, spots), jnp.bfloat16),
            pltpu.SemaphoreType.DMA((cells // size,)),
        ],
        compiler_params=params(12),
        cost_estimate=cost(cells * spots * 3, cells * spots * 4),
        name="gradient",
    )(probs, d_probs, row_dot)


def gene_sums(part, measured):
    rows, spots = part.shape
    return pl.pallas_call(
        gene_sums_kernel,
        in_specs=[VMEM] * 2,
        out_specs=[VMEM] * 2,
        out_shape=[
            jax.ShapeDtypeStruct((R, spots), jnp.float32),
            jax.ShapeDtypeStruct((3 * R, LANES), jnp.float32),
        ],
        compiler_params=params(4),
        name="gene_sums",
    )(part, measured)


def gradient_share(sums, predicted, measured):
    spots = predicted.shape[1]
    return pl.pallas_call(
        share_kernel,
        in_specs=[VMEM] * 3,
        out_specs=[VMEM] * 2,
        out_shape=[
            jax.ShapeDtypeStruct((MEMBERS * R, spots), jnp.bfloat16),
            jax.ShapeDtypeStruct((R, LANES), jnp.float32),
        ],
        compiler_params=params(4),
        name="share",
    )(sums, predicted, measured)


def body(logits, expression, measured):
    spots = logits.shape[1]
    far_logits = pltpu.with_memory_space_constraint(logits, pltpu.HBM)
    far_expression = pltpu.with_memory_space_constraint(expression, pltpu.HBM)
    local_log = local_log_sum(far_logits)
    expression_t = transposed(far_expression)
    log_total = narrow_combine(local_log, log_add)
    part = partial_predicted(far_logits, expression_t, log_total)
    part = reduce_scatter(part)
    predicted, sums = gene_sums(part, measured)
    share, cosine = gradient_share(narrow_combine(sums, jnp.add), predicted, measured)
    similarity = cosine[:, 0]
    share, log_total = lax.optimization_barrier((all_gather_second(share), log_total))
    probs, expression = probabilities(far_logits, far_expression, log_total)
    d_pred = all_gather_first(share)
    d_probs, row_dot = backward(probs, expression, d_pred)
    row_dot = narrow_combine(row_dot, jnp.add)
    grad = gradient(probs, d_probs, row_dot, float(spots * lax.axis_size("narrow")))
    return (grad, similarity)


def solution(mesh):
    placed = (P("wide", "narrow"), P("wide", None), P("wide", "narrow"))
    return jax.shard_map(
        body,
        mesh=mesh,
        in_specs=placed,
        out_specs=(P("wide", "narrow"), P("wide")),
        check_vma=False,
    )
```

```python
import functools

import jax
import jax.numpy as jnp
from jax import lax
from jax.experimental import pallas as pl
from jax.experimental.pallas import tpu as pltpu
from jax.sharding import PartitionSpec as P

Y, Z, X, R, N = 4, 8, 2, 8, 4
H, L = 4, 2
FOUR, MEMBERS = 4, 16
LANES = 128
ROWS = 256
MIB = 1 << 20


def wide_index(y, z, x):
    return (y * Z + z) * X + x


def device_index(y, z, x, n):
    return wide_index(y, z, x) * N + n


def zx_groups(n):
    return [[device_index(y, z, x, n) for z in range(Z) for x in range(X)] for y in range(Y)]


def yh_groups(n):
    return [
        [device_index(y, 2 * h + l, x, n) for y in range(Y) for h in range(H)]
        for x in range(X)
        for l in range(L)
    ]


def partner(y, z, x, n, k):
    if n % 2 == 0:
        return device_index((y + k) % Y, z, x, n)
    o = (L * x + z % L) ^ k
    return device_index(y, z - z % L + o % L, o // L, n)


FIRST = {
    k: [
        (device_index(y, z, x, n), partner(y, z, x, n, k))
        for y in range(Y)
        for z in range(Z)
        for x in range(X)
        for n in range(N)
    ]
    for k in (1, 2, 3)
}
SECOND = [g for n in range(N) for g in (yh_groups(n) if n % 2 else zx_groups(n))]
ORDER = (2, 1, 3)


def send_first(v, k):
    return lax.ppermute(v, ("wide", "narrow"), FIRST[k])


def swap_second(v):
    return lax.all_to_all(v, ("wide", "narrow"), 0, 0, axis_index_groups=SECOND)


def by_core(even, odd):
    return jnp.where(lax.axis_index("narrow") % 2 == 0, even, odd)


def own_block():
    wide = lax.axis_index("wide")
    return by_core(wide // (Z * X), (wide % X) * L + (wide // X) % L)


def reduce_scatter(part):
    spots = part.shape[1]
    blocks = by_core(
        part.reshape(FOUR, -1, spots),
        part.reshape(Y, H, L, X, R, spots)
        .transpose(3, 2, 0, 1, 4, 5)
        .reshape(FOUR, -1, spots),
    )
    own = own_block()

    def pick(i):
        return lax.dynamic_index_in_dim(blocks, i, 0, keepdims=False)

    got = [send_first(pick(by_core((own + k) % FOUR, own ^ k)), k) for k in ORDER]
    total = fold([v.astype(jnp.float32) for v in [pick(own)] + got], jnp.add)
    total = total.astype(jnp.bfloat16).reshape(MEMBERS, R, spots)
    return swap_second(total).reshape(MEMBERS * R, spots)


def all_gather_second(share):
    spots = share.shape[1]
    return swap_second(share.reshape(MEMBERS, R, spots)).reshape(MEMBERS * R, spots)


def all_gather_first(block):
    spots = block.shape[1]
    got = {k: send_first(block, k) for k in ORDER}
    got[0] = block
    own = own_block()
    blocks = jnp.stack(
        [
            lax.select_n(by_core((own - j) % FOUR, own ^ j), *[got[k] for k in range(FOUR)])
            for j in range(FOUR)
        ]
    )
    return by_core(
        blocks.reshape(-1, spots),
        blocks.reshape(X, L, Y, H, R, spots).transpose(2, 3, 1, 0, 4, 5).reshape(-1, spots),
    )


def narrow_combine(v, op):
    for d in (1, 2):
        v = op(v, lax.ppermute(v, "narrow", [(i, i ^ d) for i in range(4)]))
    return v


def log_add(a, b):
    top = jnp.maximum(a, b)
    return top + jnp.log(jnp.exp(a - top) + jnp.exp(b - top))


def fold(parts, op):
    parts = list(parts)
    while len(parts) > 1:
        parts = [op(a, b) for a, b in zip(parts[::2], parts[1::2])]
    return parts[0]


def lane_groups(width):
    return [slice(k, k + LANES) for k in range(0, width, LANES)]


def as_row(column_sums):
    return jnp.sum(column_sums.T, axis=0, keepdims=True)


def as_column(row):
    return jnp.broadcast_to(row, (LANES, row.shape[1])).T


def block(i):
    return pl.ds(pl.multiple_of(i * ROWS, ROWS), ROWS)


def stats_kernel(x_hbm, out_ref, x_ref, sems):
    cells, spots = x_ref.shape
    steps = cells // ROWS
    groups = lane_groups(spots)

    def copy(i):
        return pltpu.make_async_copy(x_hbm.at[block(i), :], x_ref.at[block(i), :], sems.at[i])

    for i in range(steps):
        copy(i).start()

    def log_sum(i):
        rows = block(i)
        top = fold([x_ref[rows, g] for g in groups], jnp.maximum).astype(jnp.float32)
        total = fold([jnp.exp(x_ref[rows, g].astype(jnp.float32) - top) for g in groups], jnp.add)
        top, total = top.T, total.T
        row_top = jnp.max(top, axis=0, keepdims=True)
        row_total = jnp.sum(total * jnp.exp(top - row_top), axis=0, keepdims=True)
        out_ref[pl.ds(i, 1), :] = row_top + jnp.log(row_total)

    @pl.loop(0, steps // 2)
    def _(i):
        copy(2 * i).wait()
        copy(2 * i + 1).wait()
        log_sum(2 * i)
        log_sum(2 * i + 1)


def transpose_kernel(e_hbm, out_ref, e_ref, sems):
    steps = e_ref.shape[0] // ROWS

    def copy(i):
        return pltpu.make_async_copy(e_hbm.at[block(i), :], e_ref.at[block(i), :], sems.at[i])

    for i in range(steps):
        copy(i).start()

    @pl.loop(0, steps)
    def _(i):
        copy(i).wait()
        out_ref[:, block(i)] = e_ref[block(i), :].T


def probs_kernel(x_hbm, e_hbm, log_ref, probs_ref, e_ref, x_ref, sems):
    cells, spots = x_ref.shape
    steps = cells // ROWS

    def copy(i):
        return pltpu.make_async_copy(x_hbm.at[block(i), :], x_ref.at[block(i), :], sems.at[i])

    for i in range(steps):
        copy(i).start()
    expression = pltpu.make_async_copy(e_hbm, e_ref, sems.at[steps])
    expression.start()

    @pl.loop(0, steps)
    def _(i):
        copy(i).wait()
        log_total = as_column(log_ref[pl.ds(i, 1), :])
        for g in lane_groups(spots):
            probs_ref[block(i), g] = jnp.exp(x_ref[block(i), g].astype(jnp.float32) - log_total)

    expression.wait()


def forward_kernel(x_hbm, et_ref, log_ref, part_ref, x_ref, low, sems):
    cells, spots = x_ref.shape
    steps = cells // ROWS

    def copy(i):
        return pltpu.make_async_copy(x_hbm.at[block(i), :], x_ref.at[block(i), :], sems.at[i])

    for i in range(steps):
        copy(i).start()

    def fill(i):
        log_total = as_column(log_ref[pl.ds(i, 1), :])
        for g in lane_groups(spots):
            probs = jnp.exp(x_ref[block(i), g].astype(jnp.float32) - log_total)
            low[block(i), g] = probs.astype(jnp.bfloat16)

    @pl.loop(0, steps // 2)
    def _(i):
        copy(2 * i).wait()
        copy(2 * i + 1).wait()
        fill(2 * i)
        fill(2 * i + 1)

    part = jnp.dot(et_ref[...], low[...], preferred_element_type=jnp.float32)
    part_ref[...] = part.astype(jnp.bfloat16)


def backward_kernel(size, probs_ref, e_ref, d_ref, dprobs_ref, dot_ref):
    cells, spots = probs_ref.shape

    def row_dots(first):
        for k in range(first, first + size, ROWS):
            rows = slice(k, k + ROWS)
            parts = [probs_ref[rows, g] * dprobs_ref[rows, g] for g in lane_groups(spots)]
            dot_ref[k // ROWS : k // ROWS + 1, :] = as_row(fold(parts, jnp.add))

    for first in range(0, cells, size):
        rows = slice(first, first + size)
        dprobs_ref[rows, :] = jnp.dot(e_ref[rows, :], d_ref[...], preferred_element_type=jnp.float32)
        if first:
            row_dots(first - size)
    row_dots(cells - size)


def gradient_kernel(scale, size, probs_ref, dprobs_ref, dot_ref, out_hbm, buf, sems):
    cells, spots = probs_ref.shape
    steps = cells // size
    inner = size // ROWS

    def copy(i):
        rows = pl.ds(pl.multiple_of(i * size, size), size)
        return pltpu.make_async_copy(buf.at[rows, :], out_hbm.at[rows, :], sems.at[i])

    @pl.loop(0, steps)
    def _(i):
        for h in range(inner):
            rows = block(i * inner + h)
            row_dot = as_column(dot_ref[pl.ds(i * inner + h, 1), :])
            for g in lane_groups(spots):
                grad = scale * probs_ref[rows, g] * (dprobs_ref[rows, g] - row_dot)
                buf[rows, g] = grad.astype(jnp.bfloat16)
        copy(i).start()

    for i in range(steps):
        copy(i).wait()


def gene_sums_kernel(part_ref, measured_ref, predicted_ref, sums_ref):
    rows = part_ref.shape[0]
    pairs = [part_ref[k : k + 2 * R, :].astype(jnp.float32) for k in range(0, rows, 2 * R)]
    pairs = fold(pairs, jnp.add)
    predicted = pairs[:R] + pairs[R:]
    predicted_ref[...] = predicted
    measured = measured_ref[...]
    groups = lane_groups(predicted.shape[1])
    for k, v in enumerate([predicted * measured, predicted * predicted, measured * measured]):
        sums_ref[k * R : (k + 1) * R, :] = fold([v[:, g] for g in groups], jnp.add)


def share_kernel(sums_ref, predicted_ref, measured_ref, share_ref, cosine_ref):
    sums = jnp.sum(sums_ref[...], axis=1, keepdims=True)
    inner, pred_sq, meas_sq = sums[:R], sums[R : 2 * R], sums[2 * R :]
    inv_p = lax.rsqrt(pred_sq + 1e-06)
    inv_m = lax.rsqrt(meas_sq + 1e-06)
    cosine = inner * (inv_p * inv_m)
    cosine_ref[...] = jnp.broadcast_to(cosine, cosine_ref.shape)
    share = cosine * inv_p * inv_p * predicted_ref[...] - inv_p * inv_m * measured_ref[...]
    share = jnp.concatenate([share, share]).astype(jnp.bfloat16)
    for k in range(0, share_ref.shape[0], 2 * R):
        share_ref[k : k + 2 * R, :] = share


VMEM = pl.BlockSpec(memory_space=pltpu.VMEM)
HBM = pl.BlockSpec(memory_space=pltpu.HBM)


def params(mib):
    return pltpu.CompilerParams(vmem_limit_bytes=mib * MIB)


def cost(flops, moved, transcendentals=0):
    return pl.CostEstimate(flops=flops, bytes_accessed=moved, transcendentals=transcendentals)


def local_log_sum(logits):
    cells, spots = logits.shape
    steps = cells // ROWS
    return pl.pallas_call(
        stats_kernel,
        in_specs=[HBM],
        out_specs=VMEM,
        out_shape=jax.ShapeDtypeStruct((steps, ROWS), jnp.float32),
        scratch_shapes=[
            pltpu.VMEM((cells, spots), logits.dtype),
            pltpu.SemaphoreType.DMA((steps,)),
        ],
        compiler_params=params(8),
        cost_estimate=cost(cells * spots * 6, cells * spots * 2, cells * spots),
        name="stats",
    )(logits)


def transposed(expression):
    cells, genes = expression.shape
    return pl.pallas_call(
        transpose_kernel,
        in_specs=[HBM],
        out_specs=VMEM,
        out_shape=jax.ShapeDtypeStruct((genes, cells), expression.dtype),
        scratch_shapes=[
            pltpu.VMEM((cells, genes), expression.dtype),
            pltpu.SemaphoreType.DMA((cells // ROWS,)),
        ],
        compiler_params=params(8),
        cost_estimate=cost(0, cells * genes * 4),
        name="transpose",
    )(expression)


def probabilities(logits, expression, log_total):
    cells, spots = logits.shape
    steps = cells // ROWS
    return pl.pallas_call(
        probs_kernel,
        in_specs=[HBM, HBM, VMEM],
        out_specs=[VMEM, VMEM],
        out_shape=[
            jax.ShapeDtypeStruct((cells, spots), jnp.float32),
            jax.ShapeDtypeStruct(expression.shape, expression.dtype),
        ],
        scratch_shapes=[
            pltpu.VMEM((cells, spots), logits.dtype),
            pltpu.SemaphoreType.DMA((steps + 1,)),
        ],
        compiler_params=params(8),
        cost_estimate=cost(cells * spots * 4, cells * spots * 4, cells * spots),
        name="probs",
    )(logits, expression, log_total)


def partial_predicted(logits, expression_t, log_total):
    cells, spots = logits.shape
    genes = expression_t.shape[0]
    return pl.pallas_call(
        forward_kernel,
        in_specs=[HBM, VMEM, VMEM],
        out_specs=VMEM,
        out_shape=jax.ShapeDtypeStruct((genes, spots), jnp.bfloat16),
        scratch_shapes=[
            pltpu.VMEM((cells, spots), jnp.bfloat16),
            pltpu.VMEM((cells, spots), jnp.bfloat16),
            pltpu.SemaphoreType.DMA((cells // ROWS,)),
        ],
        compiler_params=params(16),
        cost_estimate=cost(2 * cells * spots * genes, cells * spots * 4, cells * spots),
        name="forward",
    )(logits, expression_t, log_total)


def backward(probs, expression, d_pred):
    cells, spots = probs.shape
    genes = expression.shape[1]
    return pl.pallas_call(
        functools.partial(backward_kernel, 512),
        in_specs=[VMEM] * 3,
        out_specs=[VMEM] * 2,
        out_shape=[
            jax.ShapeDtypeStruct((cells, spots), jnp.float32),
            jax.ShapeDtypeStruct((cells // ROWS, ROWS), jnp.float32),
        ],
        compiler_params=params(8),
        cost_estimate=cost(2 * cells * spots * genes, cells * spots * 4),
        name="backward",
    )(probs, expression, d_pred)


def gradient(probs, d_probs, row_dot, scale):
    cells, spots = probs.shape
    size = 512
    return pl.pallas_call(
        functools.partial(gradient_kernel, scale, size),
        in_specs=[VMEM] * 3,
        out_specs=HBM,
        out_shape=jax.ShapeDtypeStruct((cells, spots), jnp.bfloat16),
        scratch_shapes=[
            pltpu.VMEM((cells, spots), jnp.bfloat16),
            pltpu.SemaphoreType.DMA((cells // size,)),
        ],
        compiler_params=params(12),
        cost_estimate=cost(cells * spots * 3, cells * spots * 4),
        name="gradient",
    )(probs, d_probs, row_dot)


def gene_sums(part, measured):
    rows, spots = part.shape
    return pl.pallas_call(
        gene_sums_kernel,
        in_specs=[VMEM] * 2,
        out_specs=[VMEM] * 2,
        out_shape=[
            jax.ShapeDtypeStruct((R, spots), jnp.float32),
            jax.ShapeDtypeStruct((3 * R, LANES), jnp.float32),
        ],
        compiler_params=params(4),
        name="gene_sums",
    )(part, measured)


def gradient_share(sums, predicted, measured):
    spots = predicted.shape[1]
    return pl.pallas_call(
        share_kernel,
        in_specs=[VMEM] * 3,
        out_specs=[VMEM] * 2,
        out_shape=[
            jax.ShapeDtypeStruct((MEMBERS * R, spots), jnp.bfloat16),
            jax.ShapeDtypeStruct((R, LANES), jnp.float32),
        ],
        compiler_params=params(4),
        name="share",
    )(sums, predicted, measured)


def body(logits, expression, measured):
    spots = logits.shape[1]
    far_logits = pltpu.with_memory_space_constraint(logits, pltpu.HBM)
    far_expression = pltpu.with_memory_space_constraint(expression, pltpu.HBM)
    local_log = local_log_sum(far_logits)
    expression_t = transposed(far_expression)
    log_total = narrow_combine(local_log, log_add)
    part = partial_predicted(far_logits, expression_t, log_total)
    part = reduce_scatter(part)
    predicted, sums = gene_sums(part, measured)
    share, cosine = gradient_share(narrow_combine(sums, jnp.add), predicted, measured)
    similarity = cosine[:, 0]
    share, log_total = lax.optimization_barrier((all_gather_second(share), log_total))
    probs, expression = probabilities(far_logits, far_expression, log_total)
    d_pred = all_gather_first(share)
    d_probs, row_dot = backward(probs, expression, d_pred)
    row_dot = narrow_combine(row_dot, jnp.add)
    grad = gradient(probs, d_probs, row_dot, float(spots * lax.axis_size("narrow")))
    return (grad, similarity)


def solution(mesh):
    placed = (P("wide", "narrow"), P("wide", None), P("wide", "narrow"))
    return jax.shard_map(
        body,
        mesh=mesh,
        in_specs=placed,
        out_specs=(P("wide", "narrow"), P("wide")),
        check_vma=False,
    )
```

```python
import functools

import jax
import jax.numpy as jnp
from jax import lax
from jax.experimental import pallas as pl
from jax.experimental.pallas import tpu as pltpu
from jax.sharding import PartitionSpec as P

Y, Z, X, R, N = 4, 8, 2, 8, 4
H, L = 4, 2
FOUR, MEMBERS = 4, 16
LANES = 128
ROWS = 256
MIB = 1 << 20


def wide_index(y, z, x):
    return (y * Z + z) * X + x


def device_index(y, z, x, n):
    return wide_index(y, z, x) * N + n


def zx_groups(n):
    return [[device_index(y, z, x, n) for z in range(Z) for x in range(X)] for y in range(Y)]


def yh_groups(n):
    return [
        [device_index(y, 2 * h + l, x, n) for y in range(Y) for h in range(H)]
        for x in range(X)
        for l in range(L)
    ]


def partner(y, z, x, n, k):
    if n % 2 == 0:
        return device_index((y + k) % Y, z, x, n)
    o = (L * x + z % L) ^ k
    return device_index(y, z - z % L + o % L, o // L, n)


FIRST = {
    k: [
        (device_index(y, z, x, n), partner(y, z, x, n, k))
        for y in range(Y)
        for z in range(Z)
        for x in range(X)
        for n in range(N)
    ]
    for k in (1, 2, 3)
}
SECOND = [g for n in range(N) for g in (yh_groups(n) if n % 2 else zx_groups(n))]
ORDER = (2, 1, 3)


def send_first(v, k):
    return lax.ppermute(v, ("wide", "narrow"), FIRST[k])


def swap_second(v):
    return lax.all_to_all(v, ("wide", "narrow"), 0, 0, axis_index_groups=SECOND)


def by_core(even, odd):
    return jnp.where(lax.axis_index("narrow") % 2 == 0, even, odd)


def own_block():
    wide = lax.axis_index("wide")
    return by_core(wide // (Z * X), (wide % X) * L + (wide // X) % L)


def reduce_scatter(part):
    spots = part.shape[1]
    blocks = by_core(
        part.reshape(FOUR, -1, spots),
        part.reshape(Y, H, L, X, R, spots)
        .transpose(3, 2, 0, 1, 4, 5)
        .reshape(FOUR, -1, spots),
    )
    own = own_block()

    def pick(i):
        return lax.dynamic_index_in_dim(blocks, i, 0, keepdims=False)

    got = [send_first(pick(by_core((own + k) % FOUR, own ^ k)), k) for k in ORDER]
    total = fold([v.astype(jnp.float32) for v in [pick(own)] + got], jnp.add)
    total = total.astype(jnp.bfloat16).reshape(MEMBERS, R, spots)
    return swap_second(total).reshape(MEMBERS * R, spots)


def all_gather_second(share):
    spots = share.shape[1]
    return swap_second(share.reshape(MEMBERS, R, spots)).reshape(MEMBERS * R, spots)


def all_gather_first(block):
    spots = block.shape[1]
    got = {k: send_first(block, k) for k in ORDER}
    got[0] = block
    own = own_block()
    blocks = jnp.stack(
        [
            lax.select_n(by_core((own - j) % FOUR, own ^ j), *[got[k] for k in range(FOUR)])
            for j in range(FOUR)
        ]
    )
    return by_core(
        blocks.reshape(-1, spots),
        blocks.reshape(X, L, Y, H, R, spots).transpose(2, 3, 1, 0, 4, 5).reshape(-1, spots),
    )


def narrow_combine(v, op):
    for d in (1, 2):
        v = op(v, lax.ppermute(v, "narrow", [(i, i ^ d) for i in range(4)]))
    return v


def log_add(a, b):
    top = jnp.maximum(a, b)
    return top + jnp.log(jnp.exp(a - top) + jnp.exp(b - top))


def fold(parts, op):
    parts = list(parts)
    while len(parts) > 1:
        parts = [op(a, b) for a, b in zip(parts[::2], parts[1::2])]
    return parts[0]


def lane_groups(width):
    return [slice(k, k + LANES) for k in range(0, width, LANES)]


def as_row(column_sums):
    return jnp.sum(column_sums.T, axis=0, keepdims=True)


def as_column(row):
    return jnp.broadcast_to(row, (LANES, row.shape[1])).T


def block(i):
    return pl.ds(pl.multiple_of(i * ROWS, ROWS), ROWS)


def stats_kernel(x_hbm, out_ref, x_ref, sems):
    cells, spots = x_ref.shape
    steps = cells // ROWS
    groups = lane_groups(spots)

    def copy(i):
        return pltpu.make_async_copy(x_hbm.at[block(i), :], x_ref.at[block(i), :], sems.at[i])

    for i in range(steps):
        copy(i).start()

    def log_sum(i):
        rows = block(i)
        top = fold([x_ref[rows, g] for g in groups], jnp.maximum).astype(jnp.float32)
        total = fold([jnp.exp(x_ref[rows, g].astype(jnp.float32) - top) for g in groups], jnp.add)
        top, total = top.T, total.T
        row_top = jnp.max(top, axis=0, keepdims=True)
        row_total = jnp.sum(total * jnp.exp(top - row_top), axis=0, keepdims=True)
        out_ref[pl.ds(i, 1), :] = row_top + jnp.log(row_total)

    @pl.loop(0, steps // 2)
    def _(i):
        copy(2 * i).wait()
        copy(2 * i + 1).wait()
        log_sum(2 * i)
        log_sum(2 * i + 1)


def transpose_kernel(e_hbm, out_ref, e_ref, sems):
    steps = e_ref.shape[0] // ROWS

    def copy(i):
        return pltpu.make_async_copy(e_hbm.at[block(i), :], e_ref.at[block(i), :], sems.at[i])

    for i in range(steps):
        copy(i).start()

    @pl.loop(0, steps)
    def _(i):
        copy(i).wait()
        out_ref[:, block(i)] = e_ref[block(i), :].T


def probs_kernel(x_hbm, e_hbm, log_ref, probs_ref, e_ref, x_ref, sems):
    cells, spots = x_ref.shape
    steps = cells // ROWS

    def copy(i):
        return pltpu.make_async_copy(x_hbm.at[block(i), :], x_ref.at[block(i), :], sems.at[i])

    for i in range(steps):
        copy(i).start()
    expression = pltpu.make_async_copy(e_hbm, e_ref, sems.at[steps])
    expression.start()

    @pl.loop(0, steps)
    def _(i):
        copy(i).wait()
        log_total = as_column(log_ref[pl.ds(i, 1), :])
        for g in lane_groups(spots):
            probs_ref[block(i), g] = jnp.exp(x_ref[block(i), g].astype(jnp.float32) - log_total)

    expression.wait()


def forward_kernel(size, x_hbm, et_ref, log_ref, part_ref, x_ref, low, acc, sems):
    cells, spots = x_ref.shape
    inner = size // ROWS

    def copy(i):
        return pltpu.make_async_copy(x_hbm.at[block(i), :], x_ref.at[block(i), :], sems.at[i])

    for i in range(cells // ROWS):
        copy(i).start()

    def fill(step):
        for i in range(step * inner, (step + 1) * inner):
            copy(i).wait()
        for i in range(step * inner, (step + 1) * inner):
            rows = slice(i * ROWS, (i + 1) * ROWS)
            log_total = as_column(log_ref[i : i + 1, :])
            for g in lane_groups(spots):
                probs = jnp.exp(x_ref[rows, g].astype(jnp.float32) - log_total)
                low[rows, g] = probs.astype(jnp.bfloat16)

    def partial(step):
        rows = slice(step * size, (step + 1) * size)
        return jnp.dot(et_ref[:, rows], low[rows, :], preferred_element_type=jnp.float32)

    steps = cells // size
    fill(0)
    for step in range(steps - 1):
        fill(step + 1)
        part = partial(step)
        acc[...] = part if step == 0 else acc[...] + part
    part_ref[...] = (acc[...] + partial(steps - 1)).astype(jnp.bfloat16)


def backward_kernel(size, probs_ref, e_ref, d_ref, dprobs_ref, dot_ref):
    cells, spots = probs_ref.shape

    def row_dots(first):
        for k in range(first, first + size, ROWS):
            rows = slice(k, k + ROWS)
            parts = [probs_ref[rows, g] * dprobs_ref[rows, g] for g in lane_groups(spots)]
            dot_ref[k // ROWS : k // ROWS + 1, :] = as_row(fold(parts, jnp.add))

    for first in range(0, cells, size):
        rows = slice(first, first + size)
        dprobs_ref[rows, :] = jnp.dot(e_ref[rows, :], d_ref[...], preferred_element_type=jnp.float32)
        if first:
            row_dots(first - size)
    row_dots(cells - size)


def gradient_kernel(scale, size, probs_ref, dprobs_ref, dot_ref, out_hbm, buf, sems):
    cells, spots = probs_ref.shape
    steps = cells // size
    inner = size // ROWS

    def copy(i):
        rows = pl.ds(pl.multiple_of(i * size, size), size)
        return pltpu.make_async_copy(buf.at[rows, :], out_hbm.at[rows, :], sems.at[i])

    @pl.loop(0, steps)
    def _(i):
        for h in range(inner):
            rows = block(i * inner + h)
            row_dot = as_column(dot_ref[pl.ds(i * inner + h, 1), :])
            for g in lane_groups(spots):
                grad = scale * probs_ref[rows, g] * (dprobs_ref[rows, g] - row_dot)
                buf[rows, g] = grad.astype(jnp.bfloat16)
        copy(i).start()

    for i in range(steps):
        copy(i).wait()


def gene_sums_kernel(part_ref, measured_ref, predicted_ref, sums_ref):
    rows = part_ref.shape[0]
    pairs = [part_ref[k : k + 2 * R, :].astype(jnp.float32) for k in range(0, rows, 2 * R)]
    pairs = fold(pairs, jnp.add)
    predicted = pairs[:R] + pairs[R:]
    predicted_ref[...] = predicted
    measured = measured_ref[...]
    groups = lane_groups(predicted.shape[1])
    for k, v in enumerate([predicted * measured, predicted * predicted, measured * measured]):
        sums_ref[k * R : (k + 1) * R, :] = fold([v[:, g] for g in groups], jnp.add)


def share_kernel(sums_ref, predicted_ref, measured_ref, share_ref, cosine_ref):
    sums = jnp.sum(sums_ref[...], axis=1, keepdims=True)
    inner, pred_sq, meas_sq = sums[:R], sums[R : 2 * R], sums[2 * R :]
    inv_p = lax.rsqrt(pred_sq + 1e-06)
    inv_m = lax.rsqrt(meas_sq + 1e-06)
    cosine = inner * (inv_p * inv_m)
    cosine_ref[...] = jnp.broadcast_to(cosine, cosine_ref.shape)
    share = cosine * inv_p * inv_p * predicted_ref[...] - inv_p * inv_m * measured_ref[...]
    share = jnp.concatenate([share, share]).astype(jnp.bfloat16)
    for k in range(0, share_ref.shape[0], 2 * R):
        share_ref[k : k + 2 * R, :] = share


VMEM = pl.BlockSpec(memory_space=pltpu.VMEM)
HBM = pl.BlockSpec(memory_space=pltpu.HBM)


def params(mib):
    return pltpu.CompilerParams(vmem_limit_bytes=mib * MIB)


def cost(flops, moved, transcendentals=0):
    return pl.CostEstimate(flops=flops, bytes_accessed=moved, transcendentals=transcendentals)


def local_log_sum(logits):
    cells, spots = logits.shape
    steps = cells // ROWS
    return pl.pallas_call(
        stats_kernel,
        in_specs=[HBM],
        out_specs=VMEM,
        out_shape=jax.ShapeDtypeStruct((steps, ROWS), jnp.float32),
        scratch_shapes=[
            pltpu.VMEM((cells, spots), logits.dtype),
            pltpu.SemaphoreType.DMA((steps,)),
        ],
        compiler_params=params(8),
        cost_estimate=cost(cells * spots * 6, cells * spots * 2, cells * spots),
        name="stats",
    )(logits)


def transposed(expression):
    cells, genes = expression.shape
    return pl.pallas_call(
        transpose_kernel,
        in_specs=[HBM],
        out_specs=VMEM,
        out_shape=jax.ShapeDtypeStruct((genes, cells), expression.dtype),
        scratch_shapes=[
            pltpu.VMEM((cells, genes), expression.dtype),
            pltpu.SemaphoreType.DMA((cells // ROWS,)),
        ],
        compiler_params=params(8),
        cost_estimate=cost(0, cells * genes * 4),
        name="transpose",
    )(expression)


def probabilities(logits, expression, log_total):
    cells, spots = logits.shape
    steps = cells // ROWS
    return pl.pallas_call(
        probs_kernel,
        in_specs=[HBM, HBM, VMEM],
        out_specs=[VMEM, VMEM],
        out_shape=[
            jax.ShapeDtypeStruct((cells, spots), jnp.float32),
            jax.ShapeDtypeStruct(expression.shape, expression.dtype),
        ],
        scratch_shapes=[
            pltpu.VMEM((cells, spots), logits.dtype),
            pltpu.SemaphoreType.DMA((steps + 1,)),
        ],
        compiler_params=params(8),
        cost_estimate=cost(cells * spots * 4, cells * spots * 4, cells * spots),
        name="probs",
    )(logits, expression, log_total)


def partial_predicted(logits, expression_t, log_total):
    cells, spots = logits.shape
    genes = expression_t.shape[0]
    return pl.pallas_call(
        functools.partial(forward_kernel, 512),
        in_specs=[HBM, VMEM, VMEM],
        out_specs=VMEM,
        out_shape=jax.ShapeDtypeStruct((genes, spots), jnp.bfloat16),
        scratch_shapes=[
            pltpu.VMEM((cells, spots), jnp.bfloat16),
            pltpu.VMEM((cells, spots), jnp.bfloat16),
            pltpu.VMEM((genes, spots), jnp.float32),
            pltpu.SemaphoreType.DMA((cells // ROWS,)),
        ],
        compiler_params=params(16),
        cost_estimate=cost(2 * cells * spots * genes, cells * spots * 4, cells * spots),
        name="forward",
    )(logits, expression_t, log_total)


def backward(probs, expression, d_pred):
    cells, spots = probs.shape
    genes = expression.shape[1]
    return pl.pallas_call(
        functools.partial(backward_kernel, 512),
        in_specs=[VMEM] * 3,
        out_specs=[VMEM] * 2,
        out_shape=[
            jax.ShapeDtypeStruct((cells, spots), jnp.float32),
            jax.ShapeDtypeStruct((cells // ROWS, ROWS), jnp.float32),
        ],
        compiler_params=params(8),
        cost_estimate=cost(2 * cells * spots * genes, cells * spots * 4),
        name="backward",
    )(probs, expression, d_pred)


def gradient(probs, d_probs, row_dot, scale):
    cells, spots = probs.shape
    size = 512
    return pl.pallas_call(
        functools.partial(gradient_kernel, scale, size),
        in_specs=[VMEM] * 3,
        out_specs=HBM,
        out_shape=jax.ShapeDtypeStruct((cells, spots), jnp.bfloat16),
        scratch_shapes=[
            pltpu.VMEM((cells, spots), jnp.bfloat16),
            pltpu.SemaphoreType.DMA((cells // size,)),
        ],
        compiler_params=params(12),
        cost_estimate=cost(cells * spots * 3, cells * spots * 4),
        name="gradient",
    )(probs, d_probs, row_dot)


def gene_sums(part, measured):
    rows, spots = part.shape
    return pl.pallas_call(
        gene_sums_kernel,
        in_specs=[VMEM] * 2,
        out_specs=[VMEM] * 2,
        out_shape=[
            jax.ShapeDtypeStruct((R, spots), jnp.float32),
            jax.ShapeDtypeStruct((3 * R, LANES), jnp.float32),
        ],
        compiler_params=params(4),
        name="gene_sums",
    )(part, measured)


def gradient_share(sums, predicted, measured):
    spots = predicted.shape[1]
    return pl.pallas_call(
        share_kernel,
        in_specs=[VMEM] * 3,
        out_specs=[VMEM] * 2,
        out_shape=[
            jax.ShapeDtypeStruct((MEMBERS * R, spots), jnp.bfloat16),
            jax.ShapeDtypeStruct((R, LANES), jnp.float32),
        ],
        compiler_params=params(4),
        name="share",
    )(sums, predicted, measured)


def body(logits, expression, measured):
    spots = logits.shape[1]
    far_logits = pltpu.with_memory_space_constraint(logits, pltpu.HBM)
    far_expression = pltpu.with_memory_space_constraint(expression, pltpu.HBM)
    local_log = local_log_sum(far_logits)
    expression_t = transposed(far_expression)
    log_total = narrow_combine(local_log, log_add)
    part = partial_predicted(far_logits, expression_t, log_total)
    part = reduce_scatter(part)
    predicted, sums = gene_sums(part, measured)
    share, cosine = gradient_share(narrow_combine(sums, jnp.add), predicted, measured)
    similarity = cosine[:, 0]
    share, log_total = lax.optimization_barrier((all_gather_second(share), log_total))
    probs, expression = probabilities(far_logits, far_expression, log_total)
    d_pred = all_gather_first(share)
    d_probs, row_dot = backward(probs, expression, d_pred)
    row_dot = narrow_combine(row_dot, jnp.add)
    grad = gradient(probs, d_probs, row_dot, float(spots * lax.axis_size("narrow")))
    return (grad, similarity)


def solution(mesh):
    placed = (P("wide", "narrow"), P("wide", None), P("wide", "narrow"))
    return jax.shard_map(
        body,
        mesh=mesh,
        in_specs=placed,
        out_specs=(P("wide", "narrow"), P("wide")),
        check_vma=False,
    )
```

```python
import functools

import jax
import jax.numpy as jnp
from jax import lax
from jax.experimental import pallas as pl
from jax.experimental.pallas import tpu as pltpu
from jax.sharding import PartitionSpec as P

Y, Z, X, R, N = 4, 8, 2, 8, 4
H, L = 4, 2
FOUR, MEMBERS = 4, 16
LANES = 128
ROWS = 256
MIB = 1 << 20


def wide_index(y, z, x):
    return (y * Z + z) * X + x


def device_index(y, z, x, n):
    return wide_index(y, z, x) * N + n


def zx_groups(n):
    return [[device_index(y, z, x, n) for z in range(Z) for x in range(X)] for y in range(Y)]


def yh_groups(n):
    return [
        [device_index(y, 2 * h + l, x, n) for y in range(Y) for h in range(H)]
        for x in range(X)
        for l in range(L)
    ]


def partner(y, z, x, n, k):
    if n % 2 == 0:
        return device_index((y + k) % Y, z, x, n)
    o = (L * x + z % L) ^ k
    return device_index(y, z - z % L + o % L, o // L, n)


FIRST = {
    k: [
        (device_index(y, z, x, n), partner(y, z, x, n, k))
        for y in range(Y)
        for z in range(Z)
        for x in range(X)
        for n in range(N)
    ]
    for k in (1, 2, 3)
}
SECOND = [g for n in range(N) for g in (yh_groups(n) if n % 2 else zx_groups(n))]
ORDER = (2, 1, 3)


def send_first(v, k):
    return lax.ppermute(v, ("wide", "narrow"), FIRST[k])


def swap_second(v):
    return lax.all_to_all(v, ("wide", "narrow"), 0, 0, axis_index_groups=SECOND)


def by_core(even, odd):
    return jnp.where(lax.axis_index("narrow") % 2 == 0, even, odd)


def own_block():
    wide = lax.axis_index("wide")
    return by_core(wide // (Z * X), (wide % X) * L + (wide // X) % L)


def reduce_scatter(part):
    spots = part.shape[1]
    blocks = by_core(
        part.reshape(FOUR, -1, spots),
        part.reshape(Y, H, L, X, R, spots)
        .transpose(3, 2, 0, 1, 4, 5)
        .reshape(FOUR, -1, spots),
    )
    own = own_block()

    def pick(i):
        return lax.dynamic_index_in_dim(blocks, i, 0, keepdims=False)

    got = [send_first(pick(by_core((own + k) % FOUR, own ^ k)), k) for k in ORDER]
    total = fold([v.astype(jnp.float32) for v in [pick(own)] + got], jnp.add)
    total = total.astype(jnp.bfloat16).reshape(MEMBERS, R, spots)
    return swap_second(total).reshape(MEMBERS * R, spots)


def all_gather_second(share):
    spots = share.shape[1]
    return swap_second(share.reshape(MEMBERS, R, spots)).reshape(MEMBERS * R, spots)


def all_gather_first(block):
    spots = block.shape[1]
    got = {k: send_first(block, k) for k in ORDER}
    got[0] = block
    own = own_block()
    blocks = jnp.stack(
        [
            lax.select_n(by_core((own - j) % FOUR, own ^ j), *[got[k] for k in range(FOUR)])
            for j in range(FOUR)
        ]
    )
    return by_core(
        blocks.reshape(-1, spots),
        blocks.reshape(X, L, Y, H, R, spots).transpose(2, 3, 1, 0, 4, 5).reshape(-1, spots),
    )


def narrow_combine(v, op):
    for d in (1, 2):
        v = op(v, lax.ppermute(v, "narrow", [(i, i ^ d) for i in range(4)]))
    return v


def log_add(a, b):
    top = jnp.maximum(a, b)
    return top + jnp.log(jnp.exp(a - top) + jnp.exp(b - top))


def fold(parts, op):
    parts = list(parts)
    while len(parts) > 1:
        parts = [op(a, b) for a, b in zip(parts[::2], parts[1::2])]
    return parts[0]


def lane_groups(width):
    return [slice(k, k + LANES) for k in range(0, width, LANES)]


def as_row(column_sums):
    return jnp.sum(column_sums.T, axis=0, keepdims=True)


def as_column(row):
    return jnp.broadcast_to(row, (LANES, row.shape[1])).T


def block(i):
    return pl.ds(pl.multiple_of(i * ROWS, ROWS), ROWS)


def stats_kernel(x_hbm, out_ref, x_ref, sems):
    cells, spots = x_ref.shape
    steps = cells // ROWS
    groups = lane_groups(spots)

    def copy(i):
        return pltpu.make_async_copy(x_hbm.at[block(i), :], x_ref.at[block(i), :], sems.at[i])

    for i in range(steps):
        copy(i).start()

    def log_sum(i):
        rows = block(i)
        top = fold([x_ref[rows, g] for g in groups], jnp.maximum).astype(jnp.float32)
        total = fold([jnp.exp(x_ref[rows, g].astype(jnp.float32) - top) for g in groups], jnp.add)
        top, total = top.T, total.T
        row_top = jnp.max(top, axis=0, keepdims=True)
        row_total = jnp.sum(total * jnp.exp(top - row_top), axis=0, keepdims=True)
        out_ref[pl.ds(i, 1), :] = row_top + jnp.log(row_total)

    @pl.loop(0, steps // 2)
    def _(i):
        copy(2 * i).wait()
        copy(2 * i + 1).wait()
        log_sum(2 * i)
        log_sum(2 * i + 1)


def transpose_kernel(e_hbm, out_ref, e_ref, sems):
    steps = e_ref.shape[0] // ROWS

    def copy(i):
        return pltpu.make_async_copy(e_hbm.at[block(i), :], e_ref.at[block(i), :], sems.at[i])

    for i in range(steps):
        copy(i).start()

    @pl.loop(0, steps)
    def _(i):
        copy(i).wait()
        out_ref[:, block(i)] = e_ref[block(i), :].T


def probs_kernel(x_hbm, e_hbm, log_ref, probs_ref, e_ref, x_ref, sems):
    cells, spots = x_ref.shape
    steps = cells // ROWS

    def copy(i):
        return pltpu.make_async_copy(x_hbm.at[block(i), :], x_ref.at[block(i), :], sems.at[i])

    for i in range(steps):
        copy(i).start()
    expression = pltpu.make_async_copy(e_hbm, e_ref, sems.at[steps])
    expression.start()

    @pl.loop(0, steps)
    def _(i):
        copy(i).wait()
        log_total = as_column(log_ref[pl.ds(i, 1), :])
        for g in lane_groups(spots):
            probs_ref[block(i), g] = jnp.exp(x_ref[block(i), g].astype(jnp.float32) - log_total)

    expression.wait()


def forward_kernel(size, x_hbm, et_ref, log_ref, part_ref, x_ref, low, acc, sems):
    cells, spots = x_ref.shape
    inner = size // ROWS

    def copy(i):
        return pltpu.make_async_copy(x_hbm.at[block(i), :], x_ref.at[block(i), :], sems.at[i])

    for i in range(cells // ROWS):
        copy(i).start()

    def fill(step):
        for i in range(step * inner, (step + 1) * inner):
            copy(i).wait()
        for i in range(step * inner, (step + 1) * inner):
            rows = slice(i * ROWS, (i + 1) * ROWS)
            log_total = as_column(log_ref[i : i + 1, :])
            for g in lane_groups(spots):
                probs = jnp.exp(x_ref[rows, g].astype(jnp.float32) - log_total)
                low[rows, g] = probs.astype(jnp.bfloat16)

    def partial(step):
        rows = slice(step * size, (step + 1) * size)
        return jnp.dot(et_ref[:, rows], low[rows, :], preferred_element_type=jnp.float32)

    steps = cells // size
    fill(0)
    for step in range(steps - 1):
        fill(step + 1)
        part = partial(step)
        acc[...] = part if step == 0 else acc[...] + part
    part_ref[...] = (acc[...] + partial(steps - 1)).astype(jnp.bfloat16)


def backward_kernel(size, probs_ref, e_ref, d_ref, dprobs_ref, dot_ref):
    cells, spots = probs_ref.shape

    def row_dots(first):
        for k in range(first, first + size, ROWS):
            rows = slice(k, k + ROWS)
            parts = [probs_ref[rows, g] * dprobs_ref[rows, g] for g in lane_groups(spots)]
            dot_ref[k // ROWS : k // ROWS + 1, :] = as_row(fold(parts, jnp.add))

    for first in range(0, cells, size):
        rows = slice(first, first + size)
        dprobs_ref[rows, :] = jnp.dot(e_ref[rows, :], d_ref[...], preferred_element_type=jnp.float32)
        if first:
            row_dots(first - size)
    row_dots(cells - size)


def gradient_kernel(scale, size, probs_ref, dprobs_ref, dot_ref, out_hbm, buf, sems):
    cells, spots = probs_ref.shape
    steps = cells // size
    inner = size // ROWS

    def copy(i):
        rows = pl.ds(pl.multiple_of(i * size, size), size)
        return pltpu.make_async_copy(buf.at[rows, :], out_hbm.at[rows, :], sems.at[i])

    @pl.loop(0, steps)
    def _(i):
        for h in range(inner):
            rows = block(i * inner + h)
            row_dot = as_column(dot_ref[pl.ds(i * inner + h, 1), :])
            for g in lane_groups(spots):
                grad = scale * probs_ref[rows, g] * (dprobs_ref[rows, g] - row_dot)
                buf[rows, g] = grad.astype(jnp.bfloat16)
        copy(i).start()

    for i in range(steps):
        copy(i).wait()


def gene_sums_kernel(part_ref, measured_ref, predicted_ref, sums_ref):
    rows = part_ref.shape[0]
    pairs = [part_ref[k : k + 2 * R, :].astype(jnp.float32) for k in range(0, rows, 2 * R)]
    pairs = fold(pairs, jnp.add)
    predicted = pairs[:R] + pairs[R:]
    predicted_ref[...] = predicted
    measured = measured_ref[...]
    groups = lane_groups(predicted.shape[1])
    for k, v in enumerate([predicted * measured, predicted * predicted, measured * measured]):
        sums_ref[k * R : (k + 1) * R, :] = fold([v[:, g] for g in groups], jnp.add)


def share_kernel(sums_ref, predicted_ref, measured_ref, share_ref, cosine_ref):
    sums = jnp.sum(sums_ref[...], axis=1, keepdims=True)
    inner, pred_sq, meas_sq = sums[:R], sums[R : 2 * R], sums[2 * R :]
    inv_p = lax.rsqrt(pred_sq + 1e-06)
    inv_m = lax.rsqrt(meas_sq + 1e-06)
    cosine = inner * (inv_p * inv_m)
    cosine_ref[...] = jnp.broadcast_to(cosine, cosine_ref.shape)
    share = cosine * inv_p * inv_p * predicted_ref[...] - inv_p * inv_m * measured_ref[...]
    share = jnp.concatenate([share, share]).astype(jnp.bfloat16)
    for k in range(0, share_ref.shape[0], 2 * R):
        share_ref[k : k + 2 * R, :] = share


VMEM = pl.BlockSpec(memory_space=pltpu.VMEM)
HBM = pl.BlockSpec(memory_space=pltpu.HBM)


def params(mib):
    return pltpu.CompilerParams(vmem_limit_bytes=mib * MIB)


def cost(flops, moved, transcendentals=0):
    return pl.CostEstimate(flops=flops, bytes_accessed=moved, transcendentals=transcendentals)


def local_log_sum(logits):
    cells, spots = logits.shape
    steps = cells // ROWS
    return pl.pallas_call(
        stats_kernel,
        in_specs=[HBM],
        out_specs=VMEM,
        out_shape=jax.ShapeDtypeStruct((steps, ROWS), jnp.float32),
        scratch_shapes=[
            pltpu.VMEM((cells, spots), logits.dtype),
            pltpu.SemaphoreType.DMA((steps,)),
        ],
        compiler_params=params(8),
        cost_estimate=cost(cells * spots * 6, cells * spots * 2, cells * spots),
        name="stats",
    )(logits)


def transposed(expression):
    cells, genes = expression.shape
    return pl.pallas_call(
        transpose_kernel,
        in_specs=[HBM],
        out_specs=VMEM,
        out_shape=jax.ShapeDtypeStruct((genes, cells), expression.dtype),
        scratch_shapes=[
            pltpu.VMEM((cells, genes), expression.dtype),
            pltpu.SemaphoreType.DMA((cells // ROWS,)),
        ],
        compiler_params=params(8),
        cost_estimate=cost(0, cells * genes * 4),
        name="transpose",
    )(expression)


def probabilities(logits, expression, log_total):
    cells, spots = logits.shape
    steps = cells // ROWS
    return pl.pallas_call(
        probs_kernel,
        in_specs=[HBM, HBM, VMEM],
        out_specs=[VMEM, VMEM],
        out_shape=[
            jax.ShapeDtypeStruct((cells, spots), jnp.float32),
            jax.ShapeDtypeStruct(expression.shape, expression.dtype),
        ],
        scratch_shapes=[
            pltpu.VMEM((cells, spots), logits.dtype),
            pltpu.SemaphoreType.DMA((steps + 1,)),
        ],
        compiler_params=params(8),
        cost_estimate=cost(cells * spots * 4, cells * spots * 4, cells * spots),
        name="probs",
    )(logits, expression, log_total)


def partial_predicted(logits, expression_t, log_total):
    cells, spots = logits.shape
    genes = expression_t.shape[0]
    return pl.pallas_call(
        functools.partial(forward_kernel, 256),
        in_specs=[HBM, VMEM, VMEM],
        out_specs=VMEM,
        out_shape=jax.ShapeDtypeStruct((genes, spots), jnp.bfloat16),
        scratch_shapes=[
            pltpu.VMEM((cells, spots), jnp.bfloat16),
            pltpu.VMEM((cells, spots), jnp.bfloat16),
            pltpu.VMEM((genes, spots), jnp.float32),
            pltpu.SemaphoreType.DMA((cells // ROWS,)),
        ],
        compiler_params=params(16),
        cost_estimate=cost(2 * cells * spots * genes, cells * spots * 4, cells * spots),
        name="forward",
    )(logits, expression_t, log_total)


def backward(probs, expression, d_pred):
    cells, spots = probs.shape
    genes = expression.shape[1]
    return pl.pallas_call(
        functools.partial(backward_kernel, 512),
        in_specs=[VMEM] * 3,
        out_specs=[VMEM] * 2,
        out_shape=[
            jax.ShapeDtypeStruct((cells, spots), jnp.float32),
            jax.ShapeDtypeStruct((cells // ROWS, ROWS), jnp.float32),
        ],
        compiler_params=params(8),
        cost_estimate=cost(2 * cells * spots * genes, cells * spots * 4),
        name="backward",
    )(probs, expression, d_pred)


def gradient(probs, d_probs, row_dot, scale):
    cells, spots = probs.shape
    size = 512
    return pl.pallas_call(
        functools.partial(gradient_kernel, scale, size),
        in_specs=[VMEM] * 3,
        out_specs=HBM,
        out_shape=jax.ShapeDtypeStruct((cells, spots), jnp.bfloat16),
        scratch_shapes=[
            pltpu.VMEM((cells, spots), jnp.bfloat16),
            pltpu.SemaphoreType.DMA((cells // size,)),
        ],
        compiler_params=params(12),
        cost_estimate=cost(cells * spots * 3, cells * spots * 4),
        name="gradient",
    )(probs, d_probs, row_dot)


def gene_sums(part, measured):
    rows, spots = part.shape
    return pl.pallas_call(
        gene_sums_kernel,
        in_specs=[VMEM] * 2,
        out_specs=[VMEM] * 2,
        out_shape=[
            jax.ShapeDtypeStruct((R, spots), jnp.float32),
            jax.ShapeDtypeStruct((3 * R, LANES), jnp.float32),
        ],
        compiler_params=params(4),
        name="gene_sums",
    )(part, measured)


def gradient_share(sums, predicted, measured):
    spots = predicted.shape[1]
    return pl.pallas_call(
        share_kernel,
        in_specs=[VMEM] * 3,
        out_specs=[VMEM] * 2,
        out_shape=[
            jax.ShapeDtypeStruct((MEMBERS * R, spots), jnp.bfloat16),
            jax.ShapeDtypeStruct((R, LANES), jnp.float32),
        ],
        compiler_params=params(4),
        name="share",
    )(sums, predicted, measured)


def body(logits, expression, measured):
    spots = logits.shape[1]
    far_logits = pltpu.with_memory_space_constraint(logits, pltpu.HBM)
    far_expression = pltpu.with_memory_space_constraint(expression, pltpu.HBM)
    local_log = local_log_sum(far_logits)
    expression_t = transposed(far_expression)
    log_total = narrow_combine(local_log, log_add)
    part = partial_predicted(far_logits, expression_t, log_total)
    part = reduce_scatter(part)
    predicted, sums = gene_sums(part, measured)
    share, cosine = gradient_share(narrow_combine(sums, jnp.add), predicted, measured)
    similarity = cosine[:, 0]
    share, log_total = lax.optimization_barrier((all_gather_second(share), log_total))
    probs, expression = probabilities(far_logits, far_expression, log_total)
    d_pred = all_gather_first(share)
    d_probs, row_dot = backward(probs, expression, d_pred)
    row_dot = narrow_combine(row_dot, jnp.add)
    grad = gradient(probs, d_probs, row_dot, float(spots * lax.axis_size("narrow")))
    return (grad, similarity)


def solution(mesh):
    placed = (P("wide", "narrow"), P("wide", None), P("wide", "narrow"))
    return jax.shard_map(
        body,
        mesh=mesh,
        in_specs=placed,
        out_specs=(P("wide", "narrow"), P("wide")),
        check_vma=False,
    )
```
